256 devices in a mesh: tm: 8 (over z_hi, y), height: 32 (over z_lo, x, core).
Axes of the slice: x: 4, y: 4, z: 8 (z_hi: 2, z_lo: 4; z = z_hi * 4 + z_lo), core: 2. Of those that a mesh axis runs over, the one named last changes fastest.
Arguments:
- hidden_states: bfloat16 [16, 64, 64, 512], P('tm', 'height'), may hold values from -60 to 60
- attn_gain: float32 [512], replicated, may hold values from 0.5 to 1.5
- qkv_weight: bfloat16 [512, 1536], replicated, may hold values from -0.25 to 0.25
- out_weight: bfloat16 [512, 512], replicated, may hold values from -0.25 to 0.25
- up_weight: bfloat16 [512, 512], replicated, may hold values from -0.25 to 0.25
- conv_weight: bfloat16 [3, 3, 3, 128, 128], replicated, may hold values from -0.109375 to 0.109375
- cotangent: bfloat16 [16, 128, 128, 128], P('tm', 'height'), may hold values from -6 to 6
Outputs:
- decoded: bfloat16 [16, 128, 128, 128], P('tm', 'height')
- grad_states: bfloat16 [16, 64, 64, 512], P('tm', 'height')
- grad_qkv_weight: float32 [512, 1536], P('height')
- grad_out_weight: float32 [512, 512], P('height')
- grad_up_weight: float32 [512, 512], P('height')
- grad_conv_weight: float32 [3, 3, 3, 128, 128], P(None, None, None, 'height')
The draws below stay inside these ranges and needn't reach their ends.
All inputs are finite; a program needn't handle non-finite values.
Results may differ from the reference program's by a relative error of at most 0.035.
Values may be sent and summed in bfloat16 or wider, within the bound.
A program may use at most 128 MiB of HBM per device.

```python
import jax
import jax.numpy as jnp
from jax import lax

E = 512
C = 128
WL = 64
FRAMES = 16
LAT_ROWS = 64
ROWS = 128
COLS = 128
TOKENS = 65536
VOXELS = 262144


def draw_hidden_states(key, part):
    key = jax.random.fold_in(key, 11)
    noise_key, column_key, row_key = jax.random.split(key, 3)
    full_shape = (FRAMES, LAT_ROWS, WL, E)
    noise_vals = jnp.clip(jax.random.normal(noise_key, full_shape, jnp.float32), -6.0, 6.0)
    column = jnp.exp(jax.random.uniform(column_key, (E,), jnp.float32, -1.15, 1.15))
    row_scale = jnp.exp(jax.random.uniform(row_key, (FRAMES, LAT_ROWS, WL, 1), jnp.float32, -1.15, 1.15))
    return (noise_vals * column * row_scale).astype(jnp.bfloat16)


def steps_of(key, extent, cuts, smallest, top_value):
    factor_of, own = 1.0, jax.random.fold_in(key, 6)
    for axis_at, blocks in cuts:
        draws = jnp.exp(jax.random.uniform(jax.random.fold_in(own, axis_at), (blocks,), jnp.float32, smallest / len(cuts), top_value / len(cuts)))
        factor_of = factor_of * jnp.repeat(draws, extent[axis_at] // blocks).reshape([-1 if axis == axis_at else 1 for axis in range(len(extent))])
    return factor_of


def bell_draw(stream_key, extent, scale, bound, pieces=(), kind=jnp.bfloat16):
    values = scale * jax.random.normal(stream_key, extent, jnp.float32)
    if pieces:
        values = values * steps_of(stream_key, extent, pieces, -0.22, 0.18)
    return jnp.clip(values, -bound, bound).astype(kind)


def setup_inputs(seed: int = 0) -> dict:
    key_of = jax.random.split(jax.random.key(seed), 8)
    return {
        "hidden_states": draw_hidden_states(jax.random.fold_in(key_of[7], 71), 0),
        "attn_gain": jnp.clip(1.0 + 0.1 * jax.random.normal(key_of[1], (E,), jnp.float32), 0.5, 1.5),
        "qkv_weight": bell_draw(key_of[2], (E, 3 * E), E ** -0.5, 0.25),
        "out_weight": bell_draw(key_of[3], (E, E), E ** -0.5, 0.25),
        "up_weight": bell_draw(key_of[4], (E, 4 * C), E ** -0.5, 0.25),
        "conv_weight": bell_draw(key_of[5], (3, 3, 3, C, C), (27 * C) ** -0.5, 0.109375),
        "cotangent": bell_draw(key_of[6], (FRAMES, ROWS, COLS, C), 1.0, 6.0, ((0, 8), (1, 32))),
    }


epsilon = 1e-06
highest = lax.Precision.HIGHEST

def rms_scale(raw_rows):
    return lax.rsqrt(lax.optimization_barrier(jnp.mean(raw_rows * raw_rows, axis=-1, keepdims=True)) + epsilon)

def norm_back(raw_rows, upstream):
    factor = rms_scale(raw_rows)
    unit_rows = raw_rows * factor
    return factor * (upstream - unit_rows * lax.optimization_barrier(jnp.mean(upstream * unit_rows, axis=-1, keepdims=True)))

def silu_slope(pre_act):
    gate_val = jax.nn.sigmoid(pre_act)
    return gate_val * (1.0 + pre_act * (1.0 - gate_val))

def prepare(tokens, attn_gain, qkv_weight):
    states_wide = tokens.astype(jnp.float32)
    normed = (states_wide * rms_scale(states_wide) * attn_gain).astype(jnp.bfloat16)
    joined = jnp.dot(normed, qkv_weight, preferred_element_type=jnp.float32)
    query_raw = joined[:, :E]
    key_raw = joined[:, E:2 * E]
    query = (query_raw * rms_scale(query_raw)).astype(jnp.bfloat16)
    keys = (key_raw * rms_scale(key_raw)).astype(jnp.bfloat16)
    values = joined[:, 2 * E:].astype(jnp.bfloat16)
    return (normed, query_raw, key_raw, query, keys, values)

def attend(query, keys, values, start):
    width_root = query.shape[-1] ** 0.5
    scores = jnp.einsum('fle,gle->lfg', query.astype(jnp.float32), keys.astype(jnp.float32), precision=highest) / width_root
    row_ids = start + jnp.arange(query.shape[0], dtype=jnp.int32)
    col_ids = jnp.arange(keys.shape[0], dtype=jnp.int32)
    allowed = col_ids[None, :] <= row_ids[:, None]
    weights = jnp.where(allowed[None, :, :], jnp.exp(scores), 0.0)
    probs = weights / lax.optimization_barrier(jnp.sum(weights, axis=-1, keepdims=True))
    probs_low = probs.astype(jnp.bfloat16)
    mixed = jnp.einsum('lfg,gle->fle', probs_low.astype(jnp.float32), values.astype(jnp.float32), precision=highest)
    return (mixed.astype(jnp.bfloat16), probs, probs_low)

def attend_back(query, keys, values, probs, probs_low, grad_mixed):
    width_root = query.shape[-1] ** 0.5
    grad_probs = jnp.einsum('fle,gle->lfg', grad_mixed.astype(jnp.float32), values.astype(jnp.float32), precision=highest)
    inner = lax.optimization_barrier(jnp.sum(probs * grad_probs, axis=-1, keepdims=True))
    grad_scores = (probs * (grad_probs - inner) / width_root).astype(jnp.bfloat16).astype(jnp.float32)
    grad_query = jnp.einsum('lfg,gle->fle', grad_scores, keys.astype(jnp.float32), precision=highest)
    grad_keys = jnp.einsum('lfg,fle->gle', grad_scores, query.astype(jnp.float32), precision=highest)
    grad_values = jnp.einsum('lfg,fle->gle', probs_low.astype(jnp.float32), grad_mixed.astype(jnp.float32), precision=highest)
    return (grad_query, grad_keys, grad_values)

def to_pixels(flat, frames, lat_rows, lat_cols):
    blocks = flat.reshape(frames, lat_rows, lat_cols, 2, 2, C)
    return blocks.transpose(0, 1, 3, 2, 4, 5).reshape(frames, 2 * lat_rows, 2 * lat_cols, C)

def from_pixels(pixels):
    frames, rows_all, cols_all = (pixels.shape[0], pixels.shape[1], pixels.shape[2])
    blocks = pixels.reshape(frames, rows_all // 2, 2, cols_all // 2, 2, C)
    return blocks.transpose(0, 1, 3, 2, 4, 5).reshape(-1, 4 * C)

def conv_forward(pixels, kernel):
    result = lax.conv_general_dilated(pixels[None], kernel, (1, 1, 1), ((2, 0), (1, 1), (1, 1)), dimension_numbers=('NDHWC', 'DHWIO', 'NDHWC'), precision=highest)
    return result[0]

def reference(hidden_states, attn_gain, qkv_weight, out_weight, up_weight, conv_weight, cotangent):
    tokens = hidden_states.reshape(-1, E)
    normed, query_raw, key_raw, query, keys, values = prepare(tokens, attn_gain, qkv_weight)
    seq_shape = (FRAMES, LAT_ROWS * WL, E)
    seq_query = query.reshape(seq_shape)
    seq_keys = keys.reshape(seq_shape)
    seq_values = values.reshape(seq_shape)
    mixed, probs, probs_low = attend(seq_query, seq_keys, seq_values, 0)
    mixed_flat = mixed.reshape(-1, E)
    attended = jnp.dot(mixed_flat, out_weight, preferred_element_type=jnp.float32)
    merged = (tokens.astype(jnp.float32) + attended).astype(jnp.bfloat16)
    pre_act = jnp.dot(merged, up_weight, preferred_element_type=jnp.float32)
    pixels = to_pixels(jax.nn.silu(pre_act).astype(jnp.bfloat16), FRAMES, LAT_ROWS, WL)
    conv_out, conv_pull = jax.vjp(conv_forward, pixels.astype(jnp.float32), conv_weight.astype(jnp.float32))
    decoded = conv_out.astype(jnp.bfloat16)
    grad_pixels, grad_kernel = conv_pull(cotangent.astype(jnp.float32))
    grad_pre = (from_pixels(grad_pixels) * silu_slope(pre_act)).astype(jnp.bfloat16)
    grad_up = jnp.dot(merged.T, grad_pre, preferred_element_type=jnp.float32)
    grad_merged = jnp.dot(grad_pre, up_weight.T, preferred_element_type=jnp.float32)
    grad_merged_low = grad_merged.astype(jnp.bfloat16)
    grad_out = jnp.dot(mixed_flat.T, grad_merged_low, preferred_element_type=jnp.float32)
    grad_mixed = jnp.dot(grad_merged_low, out_weight.T, preferred_element_type=jnp.float32).astype(jnp.bfloat16)
    grad_query, grad_keys, grad_values = attend_back(seq_query, seq_keys, seq_values, probs, probs_low, grad_mixed.reshape(seq_shape))
    grad_joined = jnp.concatenate([norm_back(query_raw, grad_query.reshape(-1, E)), norm_back(key_raw, grad_keys.reshape(-1, E)), grad_values.reshape(-1, E)], axis=1).astype(jnp.bfloat16)
    grad_qkv = jnp.dot(normed.T, grad_joined, preferred_element_type=jnp.float32)
    grad_normed = jnp.dot(grad_joined, qkv_weight.T, preferred_element_type=jnp.float32)
    grad_states = grad_merged + norm_back(tokens.astype(jnp.float32), grad_normed * attn_gain)
    grad_states = grad_states.astype(jnp.bfloat16).reshape(hidden_states.shape)
    token_root = TOKENS ** 0.5
    voxel_root = VOXELS ** 0.5
    return (decoded, grad_states, grad_qkv / token_root, grad_out / token_root, grad_up / token_root, grad_kernel / voxel_root)
```

```python
import jax
import jax.numpy as jnp
from jax import lax
from jax.experimental import pallas as pl
from jax.experimental.pallas import tpu as pltpu
from jax.sharding import PartitionSpec as P

E = 512
C = 128


MESH = pl.DeviceIdType.MESH
BF = jnp.bfloat16
F32 = jnp.float32


def place():
    t = lax.axis_index("tm")
    h = lax.axis_index("height")
    return t, h, lax.rem(h, 2), lax.rem(h // 2, 4), h // 8


def enter(t, h):
    barrier = pltpu.get_barrier_semaphore()
    c, x, z = lax.rem(h, 2), lax.rem(h // 2, 4), h // 8
    peers = [(lax.rem(t + k, 8), h) for k in range(1, 8)]
    peers += [(t, h + 1 - 2 * c)]
    peers += [(t, z * 8 + lax.rem(x + k, 4) * 2 + c) for k in range(1, 4)]
    peers += [(t, lax.rem(z + k, 4) * 8 + x * 2 + c) for k in range(1, 4)]
    peers += [(t, lax.rem(h + 1, 32)), (t, lax.rem(h + 31, 32))]
    for peer in peers:
        pl.semaphore_signal(barrier, inc=1, device_id=peer, device_id_type=MESH)
    pl.semaphore_wait(barrier, len(peers))


def remote(src, dst, send, recv, peer):
    return pltpu.make_async_remote_copy(
        src_ref=src, dst_ref=dst, send_sem=send, recv_sem=recv, device_id=peer, device_id_type=MESH
    )


class Reducer:
    def __init__(self, refs, where):
        self.grads, self.r1, self.r2, self.s2, self.r3, self.s3, self.r4, self.total, self.send, self.recv = refs
        self.t, self.h, self.c, self.x, self.z = where
        self.wide = self.grads.shape[-1] // 4

    def start_core(self):
        c = self.c
        self.copies = [
            remote(self.grads.at[:, :, 1 - c], self.r1, self.send.at[0], self.recv.at[0], (self.t, self.h + 1 - 2 * c))
        ]
        self.copies[0].start()

    def wait(self):
        for copy in self.copies:
            copy.wait()

    def start_x(self):
        self.wait()
        c, x, z = self.c, self.x, self.z

        def add(i, carry):
            a, b = i // 4, lax.rem(i, 4)
            both = self.grads[a, b, c].astype(F32) + self.r1[a, b].astype(F32)
            self.grads[a, b, c] = both.astype(BF)
            return carry

        lax.fori_loop(0, 16, add, 0)
        self.copies = []
        for k in range(1, 4):
            to = lax.rem(x + k, 4)
            copy = remote(
                self.grads.at[:, to, c],
                self.r2.at[k - 1],
                self.send.at[k],
                self.recv.at[k],
                (self.t, z * 8 + to * 2 + c),
            )
            copy.start()
            self.copies.append(copy)

    def start_z(self):
        self.wait()
        c, x, z = self.c, self.x, self.z

        def add(i, carry):
            both = self.grads[i, x, c].astype(F32)
            for k in range(3):
                both = both + self.r2[k, i].astype(F32)
            self.s2[i] = both.astype(BF)
            return carry

        lax.fori_loop(0, 4, add, 0)
        self.copies = []
        for k in range(1, 4):
            to = lax.rem(z + k, 4)
            copy = remote(
                self.s2.at[to], self.r3.at[k - 1], self.send.at[3 + k], self.recv.at[3 + k], (self.t, to * 8 + x * 2 + c)
            )
            copy.start()
            self.copies.append(copy)

    def start_frames(self):
        self.wait()
        both = self.s2[self.z].astype(F32)
        for k in range(3):
            both = both + self.r3[k].astype(F32)
        for i in range(8):
            self.s3[i] = both[(i // 4) * 8 : (i // 4) * 8 + 8, (i % 4) * self.wide : (i % 4 + 1) * self.wide]
        self.copies = []
        for k in range(1, 8):
            to = lax.rem(self.t + k, 8)
            copy = remote(self.s3.at[to], self.r4.at[k - 1], self.send.at[6 + k], self.recv.at[6 + k], (to, self.h))
            copy.start()
            self.copies.append(copy)

    def start_gather(self):
        self.wait()
        both = self.s3[self.t]
        for k in range(7):
            both = both + self.r4[k]
        self.total[self.t] = both
        self.copies = []
        for k in range(1, 8):
            to = lax.rem(self.t + k, 8)
            copy = remote(
                self.total.at[self.t], self.total.at[self.t], self.send.at[13 + k], self.recv.at[13 + k], (to, self.h)
            )
            copy.start()
            self.copies.append(copy)


def reducer_scratch(width, grads=True):
    shapes = [pltpu.VMEM((4, 4, 2, 16, width), BF)] if grads else []
    return shapes + [
        pltpu.VMEM((4, 4, 16, width), BF),
        pltpu.VMEM((3, 4, 16, width), BF),
        pltpu.VMEM((4, 16, width), BF),
        pltpu.VMEM((3, 16, width), BF),
        pltpu.VMEM((8, 8, width // 4), F32),
        pltpu.VMEM((7, 8, width // 4), F32),
        pltpu.VMEM((8, 8, width // 4), F32),
        pltpu.SemaphoreType.DMA((21,)),
        pltpu.SemaphoreType.DMA((21,)),
    ]


WA, WB = 2048, 1536


def write_shares(first, second, qkv_out, out_out, up_out, conv_out):
    token_scale = 1.0 / 65536.0**0.5
    voxel_scale = 1.0 / 262144.0**0.5
    for half in range(2):
        rows = pl.ds(half * 8, 8)
        for quarter in range(4):
            qkv_out[rows, pl.ds(quarter * 384, 384)] = second[half * 4 + quarter] * token_scale
        up_out[rows, :] = first[half * 4 + 2] * token_scale
        out_out[rows, :] = first[half * 4 + 3] * token_scale
        for tile in range(7):
            block = first[half * 4 + tile // 4][:, (tile % 4) * 128 : (tile % 4 + 1) * 128] * voxel_scale
            for part in range(2):
                kind = half * 2 + part
                piece = block[part * 4 : part * 4 + 4]
                if kind < 3:
                    conv_out[kind * 9 + tile] = piece
                elif tile < 6:
                    conv_out[(tile % 3) * 9 + 7 + tile // 3] = piece


SHARES = (
    jax.ShapeDtypeStruct((16, 1536), F32),
    jax.ShapeDtypeStruct((16, 512), F32),
    jax.ShapeDtypeStruct((16, 512), F32),
    jax.ShapeDtypeStruct((27, 4, 128), F32),
)


def reduce_kernel(ga_in, gb_in, qkv_out, out_out, up_out, conv_out, *scratch):
    t, h, c, x, z = place()
    first = Reducer(scratch[:10], (t, h, c, x, z))
    second = Reducer(scratch[10:20], (t, h, c, x, z))
    loads = [
        pltpu.make_async_copy(ga_in, scratch[0], scratch[20].at[0]),
        pltpu.make_async_copy(gb_in, scratch[10], scratch[20].at[1]),
    ]
    for load in loads:
        load.start()
    enter(t, h)
    for load in loads:
        load.wait()
    both = (first, second)
    for name in ("start_core", "start_x", "start_z", "start_frames", "start_gather", "wait"):
        for one in both:
            getattr(one, name)()
    write_shares(first.total, second.total, qkv_out, out_out, up_out, conv_out)


def pack_conv(grad_kernel):
    taps = jnp.concatenate([grad_kernel.reshape(27, C, C), jnp.zeros((1, C, C), F32)])
    order = [a * 9 + tile if tile < 7 else 27 for a in range(3) for tile in range(8)]
    order += [(tile % 3) * 9 + 7 + tile // 3 if tile < 6 else 27 for tile in range(8)]
    picked = jnp.stack([taps[i] for i in order]).reshape(4, 8, 32, 4, C)
    return picked.transpose(2, 0, 3, 1, 4).reshape(512, 1024)


def reduce_all(grad_qkv, grad_out, grad_up, grad_kernel):
    ga = jnp.concatenate([pack_conv(grad_kernel), grad_up, grad_out], axis=1).astype(BF).reshape(4, 4, 2, 16, WA)
    gb = grad_qkv.astype(BF).reshape(4, 4, 2, 16, WB)
    return pl.pallas_call(
        reduce_kernel,
        out_shape=SHARES,
        in_specs=[pl.BlockSpec(memory_space=pl.ANY)] * 2,
        out_specs=[pl.BlockSpec(memory_space=pltpu.VMEM)] * 4,
        scratch_shapes=reducer_scratch(WA) + reducer_scratch(WB) + [pltpu.SemaphoreType.DMA((2,))],
        compiler_params=pltpu.CompilerParams(collective_id=0, has_side_effects=True, vmem_limit_bytes=48 * 2**20),
    )(ga, gb)


epsilon = 1e-06


def from_behind(value, axis, by):
    length = lax.axis_size(axis)
    pairs = [(i, i + by) for i in range(length) if 0 <= i + by < length]
    return lax.ppermute(value, axis, pairs)


def padded_2(cells, sides, width):
    for axis, dim in sides:
        count = lax.axis_size(axis)
        ends = count - 1
        head = lax.slice_in_dim(cells, 0, width, axis=dim)
        tail = lax.slice_in_dim(cells, cells.shape[dim] - width, cells.shape[dim], axis=dim)
        cells = jnp.concatenate(
            [
                lax.ppermute(tail, axis, [(i, (i + 1) % count) for i in range(ends)]),
                cells,
                lax.ppermute(head, axis, [((i + 1) % count, i) for i in range(ends)]),
            ],
            axis=dim,
        )
    return cells


def rms_scale(raw_rows):
    return lax.rsqrt(jnp.mean(raw_rows * raw_rows, axis=-1, keepdims=True) + epsilon)


def norm_back(raw_rows, upstream):
    factor = rms_scale(raw_rows)
    unit_rows = raw_rows * factor
    return factor * (upstream - unit_rows * jnp.mean(upstream * unit_rows, axis=-1, keepdims=True))


def silu_slope(pre_act):
    gate_val = jax.nn.sigmoid(pre_act)
    return gate_val * (1.0 + pre_act * (1.0 - gate_val))


def prepare(tokens, attn_gain, qkv_weight):
    states_wide = tokens.astype(jnp.float32)
    normed = (states_wide * rms_scale(states_wide) * attn_gain).astype(jnp.bfloat16)
    joined = jnp.dot(normed, qkv_weight, preferred_element_type=jnp.float32)
    query_raw = joined[:, :E]
    key_raw = joined[:, E : 2 * E]
    query = (query_raw * rms_scale(query_raw)).astype(jnp.bfloat16)
    keys = (key_raw * rms_scale(key_raw)).astype(jnp.bfloat16)
    values = joined[:, 2 * E :].astype(jnp.bfloat16)
    return (normed, query_raw, key_raw, query, keys, values)


def attend(query, keys, values):
    width_root = query.shape[-1] ** 0.5
    scores = (
        jnp.einsum("fle,gle->lfg", query, keys, preferred_element_type=jnp.float32) / width_root
    )
    row_ids = jnp.arange(query.shape[0], dtype=jnp.int32)
    col_ids = jnp.arange(keys.shape[0], dtype=jnp.int32)
    allowed = col_ids[None, :] <= row_ids[:, None]
    weights = jnp.where(allowed[None, :, :], jnp.exp(scores), 0.0)
    probs = weights / jnp.sum(weights, axis=-1, keepdims=True)
    probs_low = probs.astype(jnp.bfloat16)
    mixed = jnp.einsum("lfg,gle->fle", probs_low, values, preferred_element_type=jnp.float32)
    return (mixed.astype(jnp.bfloat16), probs, probs_low)


def attend_back(query, keys, values, probs, probs_low, grad_mixed):
    width_root = query.shape[-1] ** 0.5
    grad_probs = jnp.einsum("fle,gle->lfg", grad_mixed, values, preferred_element_type=jnp.float32)
    inner = jnp.sum(probs * grad_probs, axis=-1, keepdims=True)
    grad_scores = (probs * (grad_probs - inner) / width_root).astype(jnp.bfloat16)
    grad_query = jnp.einsum("lfg,gle->fle", grad_scores, keys, preferred_element_type=jnp.float32)
    grad_keys = jnp.einsum("lfg,fle->gle", grad_scores, query, preferred_element_type=jnp.float32)
    grad_values = jnp.einsum(
        "lfg,fle->gle", probs_low, grad_mixed, preferred_element_type=jnp.float32
    )
    return (grad_query, grad_keys, grad_values)


def to_pixels(flat, frames, lat_rows, lat_cols):
    blocks = flat.reshape(frames, lat_rows, lat_cols, 2, 2, C)
    return blocks.transpose(0, 1, 3, 2, 4, 5).reshape(frames, 2 * lat_rows, 2 * lat_cols, C)


def from_pixels(pixels):
    frames, rows_all, cols_all = (pixels.shape[0], pixels.shape[1], pixels.shape[2])
    blocks = pixels.reshape(frames, rows_all // 2, 2, cols_all // 2, 2, C)
    return blocks.transpose(0, 1, 3, 2, 4, 5).reshape(-1, 4 * C)


def shifted_columns(padded, offsets, col_count):
    wide = jnp.pad(padded, ((0, 0), (0, 0), (1, 1), (0, 0)))
    return jnp.concatenate([wide[:, :, offset : offset + col_count] for offset in offsets], axis=-1)


def body(hidden_states, attn_gain, qkv_weight, out_weight, up_weight, conv_weight, cotangent):
    frames = hidden_states.shape[0]
    lat_rows = hidden_states.shape[1]
    lat_cols = hidden_states.shape[2]
    home_shape = (frames, lat_rows, lat_cols, E)
    tokens = hidden_states.reshape(-1, E)
    normed, query_raw, key_raw, query, keys, values = prepare(tokens, attn_gain, qkv_weight)
    seq_query, seq_keys, seq_values = (
        lax.all_to_all(query.reshape(home_shape), "tm", split_axis=2, concat_axis=0, tiled=True),
        lax.all_to_all(keys.reshape(home_shape), "tm", split_axis=2, concat_axis=0, tiled=True),
        lax.all_to_all(values.reshape(home_shape), "tm", split_axis=2, concat_axis=0, tiled=True),
    )
    seq_shape = seq_query.shape
    flat_shape = (seq_shape[0], seq_shape[1] * seq_shape[2], E)
    seq_query = seq_query.reshape(flat_shape)
    seq_keys = seq_keys.reshape(flat_shape)
    seq_values = seq_values.reshape(flat_shape)
    mixed_seq, probs, probs_low = attend(seq_query, seq_keys, seq_values)
    mixed = lax.all_to_all(
        mixed_seq.reshape(seq_shape), "tm", split_axis=0, concat_axis=2, tiled=True
    )
    mixed_flat = mixed.reshape(-1, E)
    attended = jnp.dot(mixed_flat, out_weight, preferred_element_type=jnp.float32)
    merged = (tokens.astype(jnp.float32) + attended).astype(jnp.bfloat16)
    pre_act = jnp.dot(merged, up_weight, preferred_element_type=jnp.float32)
    pixels = to_pixels(jax.nn.silu(pre_act).astype(jnp.bfloat16), frames, lat_rows, lat_cols)
    rows_dev = pixels.shape[1]
    cols_all = pixels.shape[2]
    past = from_behind(pixels, "tm", 1)
    extended = jnp.concatenate([past, pixels], axis=0)
    padded = padded_2(extended, (("height", 1),), 1)
    stacked = shifted_columns(padded, (0, 1, 2), cols_all)
    kernel = conv_weight.reshape(3, 3, 3 * C, C)
    conv_out = jnp.zeros((frames, rows_dev, cols_all, C), jnp.float32)
    kernel_terms = []
    for frame_tap in range(3):
        for row_tap in range(3):
            window = stacked[frame_tap : frame_tap + frames, row_tap : row_tap + rows_dev]
            conv_out = conv_out + jnp.einsum(
                "fhwk,ko->fhwo",
                window,
                kernel[frame_tap, row_tap],
                preferred_element_type=jnp.float32,
            )
            kernel_terms.append(
                jnp.einsum("fhwk,fhwo->ko", window, cotangent, preferred_element_type=jnp.float32)
            )
    decoded = conv_out.astype(jnp.bfloat16)
    grad_kernel = jnp.stack(kernel_terms).reshape(3, 3, 3, C, C)
    spread = jnp.zeros((frames + 2, rows_dev + 2, cols_all, 3 * C), jnp.float32)
    for frame_tap in range(3):
        for row_tap in range(3):
            term = jnp.einsum(
                "fhwo,ko->fhwk",
                cotangent,
                kernel[frame_tap, row_tap],
                preferred_element_type=jnp.float32,
            )
            spread = spread + jnp.pad(
                term, ((frame_tap, 2 - frame_tap), (row_tap, 2 - row_tap), (0, 0), (0, 0))
            )
    grad_wide = jnp.zeros((frames + 2, rows_dev + 2, cols_all + 2, C), jnp.float32)
    for col_tap in range(3):
        grad_wide = grad_wide + jnp.pad(
            spread[..., col_tap * C : (col_tap + 1) * C],
            ((0, 0), (0, 0), (col_tap, 2 - col_tap), (0, 0)),
        )
    grad_ext = grad_wide[:, :, 1 : cols_all + 1]
    later = from_behind(grad_ext[:2], "tm", -1)
    own = jnp.concatenate([grad_ext[2:frames], grad_ext[frames:] + later], axis=0)
    below = from_behind(own[:, :1], "height", -1)
    above = from_behind(own[:, -1:], "height", 1)
    inner_rows = own[:, 1:-1]
    grad_pixels = jnp.concatenate(
        [inner_rows[:, :1] + above, inner_rows[:, 1:-1], inner_rows[:, -1:] + below], axis=1
    )
    grad_pre = (from_pixels(grad_pixels) * silu_slope(pre_act)).astype(jnp.bfloat16)
    grad_up = jnp.einsum("te,tk->ek", merged, grad_pre, preferred_element_type=jnp.float32)
    grad_merged = jnp.dot(grad_pre, up_weight.T, preferred_element_type=jnp.float32)
    grad_merged_low = grad_merged.astype(jnp.bfloat16)
    grad_out = jnp.einsum(
        "te,tk->ek", mixed_flat, grad_merged_low, preferred_element_type=jnp.float32
    )
    grad_mixed = jnp.dot(grad_merged_low, out_weight.T, preferred_element_type=jnp.float32).astype(
        jnp.bfloat16
    )
    grad_mixed = grad_mixed.reshape(home_shape)
    seq_grad = lax.all_to_all(grad_mixed, "tm", split_axis=2, concat_axis=0, tiled=True)
    seq_gq, seq_gk, seq_gv = attend_back(
        seq_query, seq_keys, seq_values, probs, probs_low, seq_grad.reshape(flat_shape)
    )
    grad_query, grad_keys, grad_values = (
        lax.all_to_all(
            seq_gq.reshape(seq_shape).astype(jnp.bfloat16),
            "tm",
            split_axis=0,
            concat_axis=2,
            tiled=True,
        ).astype(jnp.float32),
        lax.all_to_all(
            seq_gk.reshape(seq_shape).astype(jnp.bfloat16),
            "tm",
            split_axis=0,
            concat_axis=2,
            tiled=True,
        ).astype(jnp.float32),
        lax.all_to_all(
            seq_gv.reshape(seq_shape).astype(jnp.bfloat16),
            "tm",
            split_axis=0,
            concat_axis=2,
            tiled=True,
        ).astype(jnp.float32),
    )
    grad_joined = jnp.concatenate(
        [
            norm_back(query_raw, grad_query.reshape(-1, E)),
            norm_back(key_raw, grad_keys.reshape(-1, E)),
            grad_values.reshape(-1, E),
        ],
        axis=1,
    ).astype(jnp.bfloat16)
    grad_qkv = jnp.einsum("te,tk->ek", normed, grad_joined, preferred_element_type=jnp.float32)
    grad_normed = jnp.dot(grad_joined, qkv_weight.T, preferred_element_type=jnp.float32)
    grad_states = grad_merged + norm_back(tokens.astype(jnp.float32), grad_normed * attn_gain)
    grad_states = grad_states.astype(jnp.bfloat16).reshape(hidden_states.shape)
    shares = reduce_all(grad_qkv, grad_out, grad_up, grad_kernel)
    return (decoded, grad_states, shares[0], shares[1], shares[2], shares[3].reshape(3, 3, 3, 4, C))


def solution(mesh):
    placed = (P("tm", "height", None, None), P(), P(), P(), P(), P(), P("tm", "height", None, None))
    return jax.shard_map(
        body,
        mesh=mesh,
        in_specs=placed,
        out_specs=(
            P("tm", "height", None, None),
            P("tm", "height", None, None),
            P("height", None),
            P("height", None),
            P("height", None),
            P(None, None, None, "height", None),
        ),
        check_vma=False,
    )
```

```python
import jax
import jax.numpy as jnp
from jax import lax
from jax.experimental import pallas as pl
from jax.experimental.pallas import tpu as pltpu
from jax.sharding import PartitionSpec as P

E = 512
C = 128
EPS = 1e-06
ROOT = 1.0 / 512.0**0.5

MESH = pl.DeviceIdType.MESH
BF = jnp.bfloat16
F32 = jnp.float32


def place():
    t = lax.axis_index("tm")
    h = lax.axis_index("height")
    return t, h, lax.rem(h, 2), lax.rem(h // 2, 4), h // 8


def enter(t, h):
    barrier = pltpu.get_barrier_semaphore()
    c, x, z = lax.rem(h, 2), lax.rem(h // 2, 4), h // 8
    peers = [(lax.rem(t + k, 8), h) for k in range(1, 8)]
    peers += [(t, h + 1 - 2 * c)]
    peers += [(t, z * 8 + lax.rem(x + k, 4) * 2 + c) for k in range(1, 4)]
    peers += [(t, lax.rem(z + k, 4) * 8 + x * 2 + c) for k in range(1, 4)]
    peers += [(t, lax.rem(h + 1, 32)), (t, lax.rem(h + 31, 32))]
    for peer in peers:
        pl.semaphore_signal(barrier, inc=1, device_id=peer, device_id_type=MESH)
    pl.semaphore_wait(barrier, len(peers))


def remote(src, dst, send, recv, peer):
    return pltpu.make_async_remote_copy(
        src_ref=src, dst_ref=dst, send_sem=send, recv_sem=recv, device_id=peer, device_id_type=MESH
    )


class Reducer:
    def __init__(self, refs, where):
        self.grads, self.r1, self.r2, self.s2, self.r3, self.s3, self.r4, self.total, self.send, self.recv = refs
        self.t, self.h, self.c, self.x, self.z = where
        self.wide = self.grads.shape[-1] // 4

    def start_core(self):
        c = self.c
        self.copies = [
            remote(self.grads.at[:, :, 1 - c], self.r1, self.send.at[0], self.recv.at[0], (self.t, self.h + 1 - 2 * c))
        ]
        self.copies[0].start()

    def wait(self):
        for copy in self.copies:
            copy.wait()

    def start_x(self):
        self.wait()
        c, x, z = self.c, self.x, self.z

        def add(i, carry):
            a, b = i // 4, lax.rem(i, 4)
            both = self.grads[a, b, c].astype(F32) + self.r1[a, b].astype(F32)
            self.grads[a, b, c] = both.astype(BF)
            return carry

        lax.fori_loop(0, 16, add, 0)
        self.copies = []
        for k in range(1, 4):
            to = lax.rem(x + k, 4)
            copy = remote(
                self.grads.at[:, to, c],
                self.r2.at[k - 1],
                self.send.at[k],
                self.recv.at[k],
                (self.t, z * 8 + to * 2 + c),
            )
            copy.start()
            self.copies.append(copy)

    def start_z(self):
        self.wait()
        c, x, z = self.c, self.x, self.z

        def add(i, carry):
            both = self.grads[i, x, c].astype(F32)
            for k in range(3):
                both = both + self.r2[k, i].astype(F32)
            self.s2[i] = both.astype(BF)
            return carry

        lax.fori_loop(0, 4, add, 0)
        self.copies = []
        for k in range(1, 4):
            to = lax.rem(z + k, 4)
            copy = remote(
                self.s2.at[to], self.r3.at[k - 1], self.send.at[3 + k], self.recv.at[3 + k], (self.t, to * 8 + x * 2 + c)
            )
            copy.start()
            self.copies.append(copy)

    def start_frames(self):
        self.wait()
        both = self.s2[self.z].astype(F32)
        for k in range(3):
            both = both + self.r3[k].astype(F32)
        for i in range(8):
            self.s3[i] = both[(i // 4) * 8 : (i // 4) * 8 + 8, (i % 4) * self.wide : (i % 4 + 1) * self.wide]
        self.copies = []
        for k in range(1, 8):
            to = lax.rem(self.t + k, 8)
            copy = remote(self.s3.at[to], self.r4.at[k - 1], self.send.at[6 + k], self.recv.at[6 + k], (to, self.h))
            copy.start()
            self.copies.append(copy)

    def start_gather(self):
        self.wait()
        both = self.s3[self.t]
        for k in range(7):
            both = both + self.r4[k]
        self.total[self.t] = both
        self.copies = []
        for k in range(1, 8):
            to = lax.rem(self.t + k, 8)
            copy = remote(
                self.total.at[self.t], self.total.at[self.t], self.send.at[13 + k], self.recv.at[13 + k], (to, self.h)
            )
            copy.start()
            self.copies.append(copy)


def reducer_scratch(width, grads=True):
    shapes = [pltpu.VMEM((4, 4, 2, 16, width), BF)] if grads else []
    return shapes + [
        pltpu.VMEM((4, 4, 16, width), BF),
        pltpu.VMEM((3, 4, 16, width), BF),
        pltpu.VMEM((4, 16, width), BF),
        pltpu.VMEM((3, 16, width), BF),
        pltpu.VMEM((8, 8, width // 4), F32),
        pltpu.VMEM((7, 8, width // 4), F32),
        pltpu.VMEM((8, 8, width // 4), F32),
        pltpu.SemaphoreType.DMA((21,)),
        pltpu.SemaphoreType.DMA((21,)),
    ]


WA, WB = 2048, 1536


def write_shares(first, second, qkv_out, out_out, up_out, conv_out):
    token_scale = 1.0 / 65536.0**0.5
    voxel_scale = 1.0 / 262144.0**0.5
    for half in range(2):
        rows = pl.ds(half * 8, 8)
        for quarter in range(4):
            qkv_out[rows, pl.ds(quarter * 384, 384)] = second[half * 4 + quarter] * token_scale
        up_out[rows, :] = first[half * 4 + 2] * token_scale
        out_out[rows, :] = first[half * 4 + 3] * token_scale
        for tile in range(7):
            block = first[half * 4 + tile // 4][:, (tile % 4) * 128 : (tile % 4 + 1) * 128] * voxel_scale
            for part in range(2):
                kind = half * 2 + part
                piece = block[part * 4 : part * 4 + 4]
                if kind < 3:
                    conv_out[kind * 9 + tile] = piece
                elif tile < 6:
                    conv_out[(tile % 3) * 9 + 7 + tile // 3] = piece


SHARES = (
    jax.ShapeDtypeStruct((16, 1536), F32),
    jax.ShapeDtypeStruct((16, 512), F32),
    jax.ShapeDtypeStruct((16, 512), F32),
    jax.ShapeDtypeStruct((27, 4, 128), F32),
)


def nn(a, b):
    return jnp.dot(a, b, preferred_element_type=F32)


def nt(a, b):
    return lax.dot_general(a, b, (((1,), (1,)), ((), ())), preferred_element_type=F32)


def tn(a, b):
    return lax.dot_general(a, b, (((0,), (0,)), ((), ())), preferred_element_type=F32)


def iota(shape, dim):
    return lax.broadcasted_iota(jnp.int32, shape, dim)


def ones_where(cond):
    return jnp.where(cond, 1.0, 0.0).astype(BF)


def swap_matrix():
    r, s = iota((256, 256), 0), iota((256, 256), 1)
    return ones_where(s == (r & 15) * 16 + (r >> 4))


def to_blocks_matrix():
    r, s = iota((128, 128), 0), iota((128, 128), 1)
    return ones_where(s == ((r >> 3) & 1) * 64 + (r >> 4) * 8 + (r & 7))


def from_blocks_matrix():
    r, s = iota((128, 128), 0), iota((128, 128), 1)
    return ones_where(s == ((r >> 3) & 7) * 16 + (r >> 6) * 8 + (r & 7))


def spread_matrix():
    r, s = iota((384, 512), 0), iota((384, 512), 1)
    channel = r & 127
    return ones_where(s == (channel >> 2) * 16 + (r >> 7) * 4 + (channel & 3))


def move(matrix, rows):
    return nn(matrix, rows).astype(BF)


def rms_scale(rows):
    return lax.rsqrt(jnp.mean(rows * rows, axis=-1, keepdims=True) + EPS)


def norm_back(rows, upstream):
    factor = rms_scale(rows)
    unit = rows * factor
    return factor * (upstream - unit * jnp.mean(upstream * unit, axis=-1, keepdims=True))


def later_frames(rows, by):
    count = rows.shape[0]
    frame = iota(rows.shape, 0) & 15
    return jnp.where(frame + by <= 15, pltpu.roll(rows, count - by, 0), 0.0)


def earlier_frames(rows, by):
    frame = iota(rows.shape, 0) & 15
    return jnp.where(frame >= by, pltpu.roll(rows, by, 0), 0.0)


class Halo:
    def __init__(self, cells, send, recv, t, h):
        self.cells, self.t, self.h = cells, t, h
        inner = pl.ds(1, 4)
        left, right = lax.rem(t + 7, 8), lax.rem(t + 1, 8)
        above, below = lax.rem(h + 31, 32), lax.rem(h + 1, 32)
        self.columns = [
            remote(cells.at[inner, 1], cells.at[inner, 17], send.at[0], recv.at[0], (left, h)),
            remote(cells.at[inner, 16], cells.at[inner, 0], send.at[1], recv.at[1], (right, h)),
        ]
        self.rows = [
            remote(cells.at[1], cells.at[5], send.at[2], recv.at[2], (t, above)),
            remote(cells.at[4], cells.at[0], send.at[3], recv.at[3], (t, below)),
        ]

    def start_columns(self):
        for copy in self.columns:
            copy.start()

    def start_rows(self):
        for copy in self.columns:
            copy.wait()
        zeros = jnp.zeros((4, 16, C), BF)

        @pl.when(self.t == 0)
        def _():
            self.cells[1:5, 0] = zeros

        @pl.when(self.t == 7)
        def _():
            self.cells[1:5, 17] = zeros

        for copy in self.rows:
            copy.start()

    def finish(self):
        for copy in self.rows:
            copy.wait()
        zeros = jnp.zeros((18, 16, C), BF)

        @pl.when(self.h == 0)
        def _():
            self.cells[0] = zeros

        @pl.when(self.h == 31)
        def _():
            self.cells[5] = zeros


def block_kernel(
    hs_in, gain_in, wqkv_in, wout_in, wup_in, wconv_in, cot_in,
    decoded_out, states_out, qkv_out, out_out, up_out, conv_out,
    hs_send, hs_recv, cot_recv, wqkv, wout, wup, wconv, wf, wb,
    cot, pix, xc, shifted, normed, q_raw, k_raw, query, keys, values, probs, mixed, merged, pre,
    grad_pre, grad_merged, grad_joined, dec_send, dec_recv, gs_send, gs_recv,
    load_sem, a2a_send, a2a_recv, halo_send, halo_recv,
    *reducers,
):
    t, h, c, x, z = place()
    first = Reducer(reducers[:10], (t, h, c, x, z))
    second = Reducer(reducers[10:], (t, h, c, x, z))
    loads = [
        pltpu.make_async_copy(src, dst, load_sem.at[i])
        for i, (src, dst) in enumerate(((wqkv_in, wqkv), (wout_in, wout), (wup_in, wup), (wconv_in, wconv)))
    ]
    for load in loads:
        load.start()
    swap = swap_matrix()

    to_blocks = to_blocks_matrix()
    for f in range(2):
        moved = move(to_blocks, hs_in[f].reshape(128, E))
        hs_send[:, f] = moved.reshape(8, 16, E)
    enter(t, h)

    def exchange(kind, src_of, dst):
        copies = []
        for k in range(1, 8):
            to = lax.rem(t + k, 8)
            copy = remote(src_of(to), dst.at[t], a2a_send.at[kind, k - 1], a2a_recv.at[kind, k - 1], (to, h))
            copy.start()
            copies.append(copy)
        return copies

    hs_copies = exchange(0, lambda to: hs_send.at[to], hs_recv)
    cot_copies = exchange(
        1, lambda to: cot_in.at[:, :, pl.ds(pl.multiple_of(to * 16, 16), 16), :], cot_recv
    )
    hs_recv[t] = hs_send[t]
    cot_recv[t] = cot_in[:, :, pl.ds(pl.multiple_of(t * 16, 16), 16), :]
    cot_halo = Halo(cot, halo_send.at[0], halo_recv.at[0], t, h)
    pix_halo = Halo(pix, halo_send.at[1], halo_recv.at[1], t, h)

    loads[3].wait()
    for a in range(3):
        for k in range(9):
            tap = wconv[a * 9 + k]
            wf[k * C : (k + 1) * C, a * C : (a + 1) * C] = tap
            wb[a * C : (a + 1) * C, k * C : (k + 1) * C] = tap
    for load in loads[:3]:
        load.wait()

    for copy in hs_copies:
        copy.wait()
    tokens = move(swap, hs_recv[...].reshape(256, E))
    hs_send[...] = tokens.reshape(8, 2, 16, E)
    wide = tokens.astype(F32)
    normed[...] = (wide * rms_scale(wide) * gain_in[...]).astype(BF)
    q_raw[...] = nn(normed[...], wqkv[:, :E])
    k_raw[...] = nn(normed[...], wqkv[:, E : 2 * E])
    values[...] = nn(normed[...], wqkv[:, 2 * E :]).astype(BF)
    raw = q_raw[...]
    query[...] = (raw * rms_scale(raw)).astype(BF)
    raw = k_raw[...]
    keys[...] = (raw * rms_scale(raw)).astype(BF)

    for copy in cot_copies:
        copy.wait()
    for r in range(4):
        cells = move(swap, cot_recv[:, :, r].reshape(256, C))
        cot[r + 1, 1:17] = cells.reshape(16, 16, C)
    cot_halo.start_columns()

    rows, cols = iota((256, 256), 0), iota((256, 256), 1)
    allowed = ((rows >> 4) == (cols >> 4)) & (cols <= rows)
    weights = jnp.where(allowed, jnp.exp(nt(query[...], keys[...]) * ROOT), 0.0)
    probs[...] = weights / jnp.sum(weights, axis=-1, keepdims=True)
    mixed[...] = nn(probs[...].astype(BF), values[...]).astype(BF)
    cot_halo.start_rows()

    tokens_wide = hs_send[...].reshape(256, E).astype(F32)
    merged[...] = (tokens_wide + nn(mixed[...], wout[...])).astype(BF)
    pre[...] = nn(merged[...], wup[...])
    act = pre[...]
    act = (act / (1.0 + jnp.exp(-act))).astype(BF)
    for i in range(2):
        for a in range(2):
            for j in range(8):
                for b in range(2):
                    at = (i * 8 + j) * 16
                    kind = (2 * a + b) * C
                    pix[2 * i + a + 1, 2 * j + b + 1] = act[at : at + 16, kind : kind + C]
    pix_halo.start_columns()

    cot_halo.finish()
    for r in range(4):
        for b in range(3):
            for k in range(3):
                at = (b * 3 + k) * C
                xc[r * 256 : (r + 1) * 256, at : at + C] = cot[r + 2 - b, 2 - k : 18 - k].reshape(256, C)
    for r in range(4):
        terms = nt(xc[r * 256 : (r + 1) * 256], wb[...])
        grad = terms[:, 2 * C :] + later_frames(terms[:, C : 2 * C], 1) + later_frames(terms[:, :C], 2)
        i, a = r // 2, r % 2
        for j in range(8):
            at = (i * 8 + j) * 16
            pre_pair = pre[at : at + 16, 2 * a * C : (2 * a + 2) * C]
            gate = 1.0 / (1.0 + jnp.exp(-pre_pair))
            slope = gate * (1.0 + pre_pair * (1.0 - gate))
            pair = jnp.concatenate([grad[2 * j * 16 : 2 * j * 16 + 16], grad[2 * j * 16 + 16 : 2 * j * 16 + 32]], axis=1)
            grad_pre[at : at + 16, 2 * a * C : (2 * a + 2) * C] = (pair * slope).astype(BF)
    pix_halo.start_rows()

    spread = spread_matrix()
    for r in range(4):
        cells = pix[r + 1, 1:17].reshape(256, C).astype(F32)
        taps = [earlier_frames(cells, 2).astype(BF), earlier_frames(cells, 1).astype(BF), cells.astype(BF)]
        shifted[r * 256 : (r + 1) * 256] = move_lanes(jnp.concatenate(taps, axis=1), spread)
    quarter = (iota((512, C), 0) >> 2) & 3
    extra = [tn(shifted[...], xc[:, k * C : (k + 1) * C]) for k in (7, 8)]
    for tile in range(7):
        total = tn(shifted[...], xc[:, tile * C : (tile + 1) * C])
        if tile < 6:
            total = jnp.where(quarter == 3, pltpu.roll(extra[tile // 3], 12 - 4 * (tile % 3), 0), total)
        first.grads[:, :, :, :, tile * C : (tile + 1) * C] = total.astype(BF).reshape(4, 4, 2, 16, C)
    first.grads[:, :, :, :, 7 * C : 8 * C] = jnp.zeros((4, 4, 2, 16, C), BF)
    first.grads[:, :, :, :, 8 * C : 12 * C] = tn(merged[...], grad_pre[...]).astype(BF).reshape(4, 4, 2, 16, E)
    grad_merged[...] = nt(grad_pre[...], wup[...])
    low = grad_merged[...].astype(BF)
    first.grads[:, :, :, :, 12 * C :] = tn(mixed[...], low).astype(BF).reshape(4, 4, 2, 16, E)
    first.start_core()

    grad_mixed = nt(low, wout[...]).astype(BF)
    grad_probs = nt(grad_mixed, values[...])
    inner = jnp.sum(probs[...] * grad_probs, axis=-1, keepdims=True)
    grad_scores = (probs[...] * (grad_probs - inner) * ROOT).astype(BF)
    grad_joined[:, :E] = norm_back(q_raw[...], nn(grad_scores, keys[...])).astype(BF)
    grad_joined[:, E : 2 * E] = norm_back(k_raw[...], tn(grad_scores, query[...])).astype(BF)
    grad_joined[:, 2 * E :] = tn(probs[...].astype(BF), grad_mixed).astype(BF)
    first.start_x()
    for part in range(3):
        at = part * E
        block = tn(normed[...], grad_joined[:, at : at + E])
        second.grads[:, :, :, :, at : at + E] = block.astype(BF).reshape(4, 4, 2, 16, E)
    second.start_core()

    grad_normed = nt(grad_joined[...], wqkv[...])
    states = norm_back(hs_send[...].reshape(256, E).astype(F32), grad_normed * gain_in[...])
    states = (grad_merged[...] + states).astype(BF)
    gs_send[...] = move(swap, states).reshape(8, 2, 16, E)
    gs_copies = exchange(2, lambda to: gs_send.at[to], gs_recv)
    gs_recv[t] = gs_send[t]
    second.start_x()
    first.start_z()

    pix_halo.finish()
    for r in range(4):
        taps = [pix[r + b, k : k + 16].reshape(256, C) for b in range(3) for k in range(3)]
        terms = nn(jnp.concatenate(taps, axis=1), wf[...])
        cells = terms[:, 2 * C :] + earlier_frames(terms[:, C : 2 * C], 1) + earlier_frames(terms[:, :C], 2)
        dec_send[:, :, r] = move(swap, cells.astype(BF)).reshape(8, 2, 16, C)
    dec_copies = exchange(3, lambda to: dec_send.at[to], dec_recv)
    dec_recv[t] = dec_send[t]

    second.start_z()
    first.start_frames()
    second.start_frames()
    first.start_gather()
    second.start_gather()
    for copy in gs_copies:
        copy.wait()
    from_blocks = from_blocks_matrix()
    for f in range(2):
        states_out[f] = move(from_blocks, gs_recv[:, f].reshape(128, E)).reshape(2, 64, E)
    for copy in dec_copies:
        copy.wait()
    for k in range(8):
        decoded_out[:, :, k * 16 : (k + 1) * 16, :] = dec_recv[k]
    first.wait()
    second.wait()
    write_shares(first.total, second.total, qkv_out, out_out, up_out, conv_out)


def move_lanes(rows, matrix):
    return nn(rows, matrix).astype(BF)


def body(hidden_states, attn_gain, qkv_weight, out_weight, up_weight, conv_weight, cotangent):
    vmem = pl.BlockSpec(memory_space=pltpu.VMEM)
    hbm = pl.BlockSpec(memory_space=pl.ANY)
    scratch = [
        pltpu.VMEM((8, 2, 16, E), BF),
        pltpu.VMEM((8, 2, 16, E), BF),
        pltpu.VMEM((8, 2, 4, 16, C), BF),
        pltpu.VMEM((E, 3 * E), BF),
        pltpu.VMEM((E, E), BF),
        pltpu.VMEM((E, E), BF),
        pltpu.VMEM((27, C, C), BF),
        pltpu.VMEM((9 * C, 3 * C), BF),
        pltpu.VMEM((3 * C, 9 * C), BF),
        pltpu.VMEM((6, 18, 16, C), BF),
        pltpu.VMEM((6, 18, 16, C), BF),
        pltpu.VMEM((1024, 9 * C), BF),
        pltpu.VMEM((1024, E), BF),
        pltpu.VMEM((256, E), BF),
        pltpu.VMEM((256, E), F32),
        pltpu.VMEM((256, E), F32),
        pltpu.VMEM((256, E), BF),
        pltpu.VMEM((256, E), BF),
        pltpu.VMEM((256, E), BF),
        pltpu.VMEM((256, 256), F32),
        pltpu.VMEM((256, E), BF),
        pltpu.VMEM((256, E), BF),
        pltpu.VMEM((256, E), F32),
        pltpu.VMEM((256, E), BF),
        pltpu.VMEM((256, E), F32),
        pltpu.VMEM((256, 3 * E), BF),
        pltpu.VMEM((8, 2, 4, 16, C), BF),
        pltpu.VMEM((8, 2, 4, 16, C), BF),
        pltpu.VMEM((8, 2, 16, E), BF),
        pltpu.VMEM((8, 2, 16, E), BF),
        pltpu.SemaphoreType.DMA((4,)),
        pltpu.SemaphoreType.DMA((4, 7)),
        pltpu.SemaphoreType.DMA((4, 7)),
        pltpu.SemaphoreType.DMA((2, 4)),
        pltpu.SemaphoreType.DMA((2, 4)),
    ]
    decoded, states, qkv, out, up, conv = pl.pallas_call(
        block_kernel,
        out_shape=(
            jax.ShapeDtypeStruct(cotangent.shape, BF),
            jax.ShapeDtypeStruct(hidden_states.shape, BF),
        )
        + SHARES,
        in_specs=[vmem, vmem, hbm, hbm, hbm, hbm, vmem],
        out_specs=[vmem] * 6,
        scratch_shapes=scratch + reducer_scratch(WA) + reducer_scratch(WB),
        compiler_params=pltpu.CompilerParams(
            collective_id=0, has_side_effects=True, vmem_limit_bytes=56 * 2**20
        ),
    )(
        hidden_states,
        attn_gain.reshape(1, E),
        qkv_weight,
        out_weight,
        up_weight,
        conv_weight.reshape(27, C, C),
        cotangent,
    )
    return (decoded, states, qkv, out, up, conv.reshape(3, 3, 3, 4, C))


def solution(mesh):
    placed = (P("tm", "height", None, None), P(), P(), P(), P(), P(), P("tm", "height", None, None))
    return jax.shard_map(
        body,
        mesh=mesh,
        in_specs=placed,
        out_specs=(
            P("tm", "height", None, None),
            P("tm", "height", None, None),
            P("height", None),
            P("height", None),
            P("height", None),
            P(None, None, None, "height", None),
        ),
        check_vma=False,
    )
```

```python
import jax
import jax.numpy as jnp
from jax import lax
from jax.experimental import pallas as pl
from jax.experimental.pallas import tpu as pltpu
from jax.sharding import PartitionSpec as P

E = 512
C = 128
EPS = 1e-06
ROOT = 1.0 / 512.0**0.5

MESH = pl.DeviceIdType.MESH
BF = jnp.bfloat16
F32 = jnp.float32


def place():
    t = lax.axis_index("tm")
    h = lax.axis_index("height")
    return t, h, lax.rem(h, 2), lax.rem(h // 2, 4), h // 8


def enter(t, h):
    barrier = pltpu.get_barrier_semaphore()
    c, x, z = lax.rem(h, 2), lax.rem(h // 2, 4), h // 8
    y, far = lax.rem(t, 4), t // 4
    peers = [(lax.rem(t + k, 8), h) for k in range(1, 8)]
    peers += [(t, h + 1 - 2 * c)]
    peers += [(t, z * 8 + lax.rem(x + k, 4) * 2 + c) for k in range(1, 4)]
    for k in range(1, 8):
        to = lax.rem(far * 4 + z + k, 8)
        peers += [(to // 4 * 4 + y, lax.rem(to, 4) * 8 + x * 2 + c)]
    peers += [(lax.rem(t + i, 8), lax.rem(h + j, 32)) for i in (7, 0, 1) for j in (31, 1)]
    for peer in peers:
        pl.semaphore_signal(barrier, inc=1, device_id=peer, device_id_type=MESH)
    pl.semaphore_wait(barrier, len(peers))


def remote(src, dst, send, recv, peer):
    return pltpu.make_async_remote_copy(
        src_ref=src, dst_ref=dst, send_sem=send, recv_sem=recv, device_id=peer, device_id_type=MESH
    )


class Reducer:
    def __init__(self, refs, where):
        self.grads, self.r1, self.r2x, self.r2y, self.s2x, self.s2y, self.r3x, self.r3y = refs[:8]
        self.s3, self.r4, self.total, self.send, self.recv = refs[8:]
        self.t, self.h, self.c, self.x, self.z = where
        self.y, self.far = lax.rem(self.t, 4), self.t // 4
        self.wide = self.grads.shape[-1] // 4
        self.copies = []

    def start(self, index, src, dst, peer):
        copy = remote(src, dst, self.send.at[index], self.recv.at[index], peer)
        copy.start()
        self.copies.append(copy)

    def wait(self):
        for copy in self.copies:
            copy.wait()
        self.copies = []

    def x_peer(self, to):
        return (self.t, self.z * 8 + to * 2 + self.c)

    def y_peer(self, to):
        return (self.far * 4 + to, self.h)

    def start_core(self):
        c = self.c
        self.start(0, self.grads.at[:, :, 1 - c], self.r1, (self.t, self.h + 1 - 2 * c))

    def start_first(self):
        self.wait()
        c, wide = self.c, self.wide

        def add(i, carry):
            a, b = i // 4, lax.rem(i, 4)
            both = self.grads[a, b, c].astype(F32) + self.r1[a, b].astype(F32)
            self.grads[a, b, c] = both.astype(BF)
            return carry

        lax.fori_loop(0, 16, add, 0)
        for k in range(1, 4):
            to = lax.rem(self.x + k, 4)
            self.start(k, self.grads.at[pl.ds(0, 2), to, c], self.r2x.at[k - 1], self.x_peer(to))
            to = lax.rem(self.y + k, 4)
            columns = pl.ds(pl.multiple_of(to * wide, 128), wide)
            self.start(3 + k, self.grads.at[pl.ds(2, 2), :, c, :, columns], self.r2y.at[k - 1], self.y_peer(to))

    def start_second(self):
        self.wait()
        c, wide = self.c, self.wide
        for i in range(2):
            both = self.grads[i, self.x, c].astype(F32)
            for k in range(3):
                both = both + self.r2x[k, i].astype(F32)
            both = both.astype(BF)
            for q in range(4):
                self.s2x[q, i] = both[:, q * wide : (q + 1) * wide]
        columns = pl.ds(pl.multiple_of(self.y * wide, 128), wide)
        for i in range(2):
            for q in range(4):
                both = self.grads[2 + i, q, c, :, columns].astype(F32)
                for k in range(3):
                    both = both + self.r2y[k, i, q].astype(F32)
                self.s2y[q, i] = both.astype(BF)
        for k in range(1, 4):
            to = lax.rem(self.y + k, 4)
            self.start(6 + k, self.s2x.at[to], self.r3x.at[k - 1], self.y_peer(to))
            to = lax.rem(self.x + k, 4)
            self.start(9 + k, self.s2y.at[to], self.r3y.at[k - 1], self.x_peer(to))

    def start_rows(self):
        self.wait()
        for i in range(4):
            mine, parts = (self.s2x[self.y, i], self.r3x) if i < 2 else (self.s2y[self.x, i - 2], self.r3y)
            both = mine.astype(F32)
            for k in range(3):
                both = both + parts[k, i % 2].astype(F32)
            both = both.astype(BF)
            if self.wide == 384:
                both = jnp.concatenate([both, jnp.zeros((16, 128), BF)], axis=1)
            for q in range(2):
                self.s3[i, q] = both[:, q * 256 : (q + 1) * 256]
        for k in range(1, 8):
            to = lax.rem(self.far * 4 + self.z + k, 8)
            far, z = to // 4, lax.rem(to, 4)
            peer = (far * 4 + self.y, z * 8 + self.x * 2 + self.c)
            self.start(12 + k, self.s3.at[z, far], self.r4.at[k - 1], peer)

    def start_gather(self):
        self.wait()
        both = self.s3[self.z, self.far].astype(F32)
        for k in range(7):
            both = both + self.r4[k].astype(F32)
        self.total[self.t] = both.astype(BF)
        for k in range(1, 8):
            to = lax.rem(self.t + k, 8)
            self.start(19 + k, self.total.at[self.t], self.total.at[self.t], (to, self.h))


def reducer_scratch(width):
    wide = width // 4
    return [
        pltpu.VMEM((4, 4, 2, 16, width), BF),
        pltpu.VMEM((4, 4, 16, width), BF),
        pltpu.VMEM((3, 2, 16, width), BF),
        pltpu.VMEM((3, 2, 4, 16, wide), BF),
        pltpu.VMEM((4, 2, 16, wide), BF),
        pltpu.VMEM((4, 2, 16, wide), BF),
        pltpu.VMEM((3, 2, 16, wide), BF),
        pltpu.VMEM((3, 2, 16, wide), BF),
        pltpu.VMEM((4, 2, 16, 256), BF),
        pltpu.VMEM((7, 16, 256), BF),
        pltpu.VMEM((8, 16, 256), BF),
        pltpu.SemaphoreType.DMA((27,)),
        pltpu.SemaphoreType.DMA((27,)),
    ]


def nn(a, b):
    return jnp.dot(a, b, preferred_element_type=F32)


def nt(a, b):
    return lax.dot_general(a, b, (((1,), (1,)), ((), ())), preferred_element_type=F32)


def tn(a, b):
    return lax.dot_general(a, b, (((0,), (0,)), ((), ())), preferred_element_type=F32)


def iota(shape, dim):
    return lax.broadcasted_iota(jnp.int32, shape, dim)


def ones_where(cond):
    return jnp.where(cond, 1.0, 0.0).astype(BF)


def swap_matrix():
    r, s = iota((256, 256), 0), iota((256, 256), 1)
    return ones_where(s == (r & 15) * 16 + (r >> 4))


def to_blocks_matrix():
    r, s = iota((128, 128), 0), iota((128, 128), 1)
    return ones_where(s == ((r >> 3) & 1) * 64 + (r >> 4) * 8 + (r & 7))


def from_blocks_matrix():
    r, s = iota((128, 128), 0), iota((128, 128), 1)
    return ones_where(s == ((r >> 3) & 7) * 16 + (r >> 6) * 8 + (r & 7))


def spread_matrix():
    r, s = iota((384, 512), 0), iota((384, 512), 1)
    channel = r & 127
    return ones_where(s == (channel >> 2) * 16 + (r >> 7) * 4 + (channel & 3))


def move(matrix, rows):
    return nn(matrix, rows).astype(BF)


def rms_scale(rows):
    return lax.rsqrt(jnp.mean(rows * rows, axis=-1, keepdims=True) + EPS)


def norm_back(rows, upstream):
    factor = rms_scale(rows)
    unit = rows * factor
    return factor * (upstream - unit * jnp.mean(upstream * unit, axis=-1, keepdims=True))


def later_frames(rows, by):
    count = rows.shape[0]
    frame = iota(rows.shape, 0) & 15
    return jnp.where(frame + by <= 15, pltpu.roll(rows, count - by, 0), 0.0)


def earlier_frames(rows, by):
    frame = iota(rows.shape, 0) & 15
    return jnp.where(frame >= by, pltpu.roll(rows, by, 0), 0.0)


def move_lanes(rows, matrix):
    return nn(rows, matrix).astype(BF)


class Halo:
    def __init__(self, cells, send, recv, t, h):
        self.cells, self.t, self.h = cells, t, h
        inner = {-1: (pl.ds(1, 1), pl.ds(1, 1)), 0: (pl.ds(1, 4), pl.ds(1, 16)), 1: (pl.ds(4, 1), pl.ds(16, 1))}
        outer = {-1: (pl.ds(5, 1), pl.ds(17, 1)), 0: (pl.ds(1, 4), pl.ds(1, 16)), 1: (pl.ds(0, 1), pl.ds(0, 1))}
        self.copies = []
        for i in (-1, 0, 1):
            for j in (-1, 0, 1):
                if i or j:
                    at = len(self.copies)
                    peer = (lax.rem(t + 8 + j, 8), lax.rem(h + 32 + i, 32))
                    src = cells.at[inner[i][0], inner[j][1]]
                    dst = cells.at[outer[i][0], outer[j][1]]
                    self.copies.append(remote(src, dst, send.at[at], recv.at[at], peer))

    def start(self):
        for copy in self.copies:
            copy.start()

    def finish(self):
        for copy in self.copies:
            copy.wait()
        side, edge = jnp.zeros((6, 16, C), BF), jnp.zeros((18, 16, C), BF)

        @pl.when(self.t == 0)
        def _():
            self.cells[:, 0] = side

        @pl.when(self.t == 7)
        def _():
            self.cells[:, 17] = side

        @pl.when(self.h == 0)
        def _():
            self.cells[0] = edge

        @pl.when(self.h == 31)
        def _():
            self.cells[5] = edge


def block_kernel(
    hs_in, gain_in, wqkv_in, wout_in, wup_in, wconv_in, cot_in,
    dec_out, states_out, first_out, second_out,
    hs_send, hs_recv, cot_recv, wqkv, wout, wup, wconv, wf, wb,
    cot, pix, xc, shifted, normed, q_raw, k_raw, query, keys, values, probs, mixed, merged, pre,
    grad_pre, grad_merged, grad_joined, dec_send, dec_recv, gs_send, gs_recv,
    load_sem, a2a_send, a2a_recv, halo_send, halo_recv,
    *reducers,
):
    t, h, c, x, z = place()
    first = Reducer(reducers[:13], (t, h, c, x, z))
    second = Reducer(reducers[13:], (t, h, c, x, z))
    loads = [
        pltpu.make_async_copy(src, dst, load_sem.at[i])
        for i, (src, dst) in enumerate(((wqkv_in, wqkv), (wout_in, wout), (wup_in, wup), (wconv_in, wconv)))
    ]
    for load in loads:
        load.start()
    swap = swap_matrix()

    to_blocks = to_blocks_matrix()
    for f in range(2):
        moved = move(to_blocks, hs_in[f].reshape(128, E))
        hs_send[:, f] = moved.reshape(8, 16, E)
    enter(t, h)

    def exchange(kind, src_of, dst):
        copies = []
        for k in range(1, 8):
            to = lax.rem(t + k, 8)
            copy = remote(src_of(to), dst.at[t], a2a_send.at[kind, k - 1], a2a_recv.at[kind, k - 1], (to, h))
            copy.start()
            copies.append(copy)
        return copies

    hs_copies = exchange(0, lambda to: hs_send.at[to], hs_recv)
    cot_copies = exchange(
        1, lambda to: cot_in.at[:, :, pl.ds(pl.multiple_of(to * 16, 16), 16), :], cot_recv
    )
    hs_recv[t] = hs_send[t]
    cot_recv[t] = cot_in[:, :, pl.ds(pl.multiple_of(t * 16, 16), 16), :]
    cot_halo = Halo(cot, halo_send.at[0], halo_recv.at[0], t, h)
    pix_halo = Halo(pix, halo_send.at[1], halo_recv.at[1], t, h)

    loads[3].wait()
    for a in range(3):
        for k in range(9):
            tap = wconv[a * 9 + k]
            wf[k * C : (k + 1) * C, a * C : (a + 1) * C] = tap
            wb[a * C : (a + 1) * C, k * C : (k + 1) * C] = tap
    for load in loads[:3]:
        load.wait()

    for copy in hs_copies:
        copy.wait()
    tokens = move(swap, hs_recv[...].reshape(256, E))
    hs_send[...] = tokens.reshape(8, 2, 16, E)
    wide = tokens.astype(F32)
    normed[...] = (wide * rms_scale(wide) * gain_in[...]).astype(BF)
    q_raw[...] = nn(normed[...], wqkv[:, :E])
    k_raw[...] = nn(normed[...], wqkv[:, E : 2 * E])
    values[...] = nn(normed[...], wqkv[:, 2 * E :]).astype(BF)
    raw = q_raw[...]
    query[...] = (raw * rms_scale(raw)).astype(BF)
    raw = k_raw[...]
    keys[...] = (raw * rms_scale(raw)).astype(BF)

    for copy in cot_copies:
        copy.wait()
    for r in range(4):
        cells = move(swap, cot_recv[:, :, r].reshape(256, C))
        cot[r + 1, 1:17] = cells.reshape(16, 16, C)
    cot_halo.start()

    rows, cols = iota((256, 256), 0), iota((256, 256), 1)
    allowed = ((rows >> 4) == (cols >> 4)) & (cols <= rows)
    weights = jnp.where(allowed, jnp.exp(nt(query[...], keys[...]) * ROOT), 0.0)
    probs[...] = weights / jnp.sum(weights, axis=-1, keepdims=True)
    mixed[...] = nn(probs[...].astype(BF), values[...]).astype(BF)

    tokens_wide = hs_send[...].reshape(256, E).astype(F32)
    merged[...] = (tokens_wide + nn(mixed[...], wout[...])).astype(BF)
    pre[...] = nn(merged[...], wup[...])
    act = pre[...]
    act = (act / (1.0 + jnp.exp(-act))).astype(BF)
    for i in range(2):
        for a in range(2):
            for j in range(8):
                for b in range(2):
                    at = (i * 8 + j) * 16
                    kind = (2 * a + b) * C
                    pix[2 * i + a + 1, 2 * j + b + 1] = act[at : at + 16, kind : kind + C]
    pix_halo.start()

    spread = spread_matrix()
    for r in range(4):
        cells = pix[r + 1, 1:17].reshape(256, C).astype(F32)
        taps = [earlier_frames(cells, 2).astype(BF), earlier_frames(cells, 1).astype(BF), cells.astype(BF)]
        shifted[r * 256 : (r + 1) * 256] = move_lanes(jnp.concatenate(taps, axis=1), spread)
    cot_halo.finish()
    for r in range(4):
        for b in range(3):
            for k in range(3):
                at = (b * 3 + k) * C
                xc[r * 256 : (r + 1) * 256, at : at + C] = cot[r + 2 - b, 2 - k : 18 - k].reshape(256, C)
    for r in range(4):
        terms = nt(xc[r * 256 : (r + 1) * 256], wb[...])
        grad = terms[:, 2 * C :] + later_frames(terms[:, C : 2 * C], 1) + later_frames(terms[:, :C], 2)
        i, a = r // 2, r % 2
        for j in range(8):
            at = (i * 8 + j) * 16
            pre_pair = pre[at : at + 16, 2 * a * C : (2 * a + 2) * C]
            gate = 1.0 / (1.0 + jnp.exp(-pre_pair))
            slope = gate * (1.0 + pre_pair * (1.0 - gate))
            pair = jnp.concatenate([grad[2 * j * 16 : 2 * j * 16 + 16], grad[2 * j * 16 + 16 : 2 * j * 16 + 32]], axis=1)
            grad_pre[at : at + 16, 2 * a * C : (2 * a + 2) * C] = (pair * slope).astype(BF)

    quarter = (iota((512, C), 0) >> 2) & 3
    extra = [tn(shifted[...], xc[:, k * C : (k + 1) * C]) for k in (7, 8)]
    for tile in range(7):
        total = tn(shifted[...], xc[:, tile * C : (tile + 1) * C])
        if tile < 6:
            total = jnp.where(quarter == 3, pltpu.roll(extra[tile // 3], 12 - 4 * (tile % 3), 0), total)
        first.grads[:, :, :, :, tile * C : (tile + 1) * C] = total.astype(BF).reshape(4, 4, 2, 16, C)
    first.grads[:, :, :, :, 7 * C : 8 * C] = jnp.zeros((4, 4, 2, 16, C), BF)
    first.grads[:, :, :, :, 8 * C : 12 * C] = tn(merged[...], grad_pre[...]).astype(BF).reshape(4, 4, 2, 16, E)
    grad_merged[...] = nt(grad_pre[...], wup[...])
    low = grad_merged[...].astype(BF)
    first.grads[:, :, :, :, 12 * C :] = tn(mixed[...], low).astype(BF).reshape(4, 4, 2, 16, E)
    first.start_core()

    grad_mixed = nt(low, wout[...]).astype(BF)
    grad_probs = nt(grad_mixed, values[...])
    inner = jnp.sum(probs[...] * grad_probs, axis=-1, keepdims=True)
    grad_scores = (probs[...] * (grad_probs - inner) * ROOT).astype(BF)
    grad_joined[:, :E] = norm_back(q_raw[...], nn(grad_scores, keys[...])).astype(BF)
    grad_joined[:, E : 2 * E] = norm_back(k_raw[...], tn(grad_scores, query[...])).astype(BF)
    grad_joined[:, 2 * E :] = tn(probs[...].astype(BF), grad_mixed).astype(BF)
    first.start_first()
    for part in range(3):
        at = part * E
        block = tn(normed[...], grad_joined[:, at : at + E])
        second.grads[:, :, :, :, at : at + E] = block.astype(BF).reshape(4, 4, 2, 16, E)
    second.start_core()

    grad_normed = nt(grad_joined[...], wqkv[...])
    states = norm_back(hs_send[...].reshape(256, E).astype(F32), grad_normed * gain_in[...])
    states = (grad_merged[...] + states).astype(BF)
    gs_send[...] = move(swap, states).reshape(8, 2, 16, E)
    gs_copies = exchange(2, lambda to: gs_send.at[to], gs_recv)
    gs_recv[t] = gs_send[t]
    second.start_first()
    first.start_second()

    pix_halo.finish()
    for r in range(4):
        taps = [pix[r + b, k : k + 16].reshape(256, C) for b in range(3) for k in range(3)]
        terms = nn(jnp.concatenate(taps, axis=1), wf[...])
        cells = terms[:, 2 * C :] + earlier_frames(terms[:, C : 2 * C], 1) + earlier_frames(terms[:, :C], 2)
        dec_send[:, :, r] = move(swap, cells.astype(BF)).reshape(8, 2, 16, C)
    dec_copies = exchange(3, lambda to: dec_send.at[to], dec_recv)
    dec_recv[t] = dec_send[t]

    second.start_second()
    first.start_rows()
    second.start_rows()
    first.start_gather()
    second.start_gather()
    for copy in gs_copies:
        copy.wait()
    states_out[...] = gs_recv[...]
    for copy in dec_copies:
        copy.wait()
    dec_out[...] = dec_recv[...]
    first.wait()
    second.wait()
    first_out[...] = first.total[...]
    second_out[...] = second.total[...]


WA, WB = 2048, 1536
SHARES = (
    jax.ShapeDtypeStruct((16, 1536), F32),
    jax.ShapeDtypeStruct((16, 512), F32),
    jax.ShapeDtypeStruct((16, 512), F32),
    jax.ShapeDtypeStruct((27, 4, 128), F32),
)


def finish_kernel(dec, states, first, second, decoded_out, states_out, qkv_out, out_out, up_out, conv_out):
    token_scale = 1.0 / 65536.0**0.5
    voxel_scale = 1.0 / 262144.0**0.5
    from_blocks = from_blocks_matrix()
    for f in range(2):
        states_out[f] = move(from_blocks, states[:, f].reshape(128, E)).reshape(2, 64, E)
    for k in range(8):
        decoded_out[:, :, k * 16 : (k + 1) * 16, :] = dec[k]

    def tile_of(total, tile, count):
        y, inner = tile // count, tile % count
        return total[(inner // 2) * 4 + y][:, (inner % 2) * 128 : (inner % 2 + 1) * 128].astype(F32)

    for tile in range(12):
        qkv_out[:, tile * 128 : (tile + 1) * 128] = tile_of(second, tile, 3) * token_scale
    for tile in range(4):
        up_out[:, tile * 128 : (tile + 1) * 128] = tile_of(first, 8 + tile, 4) * token_scale
        out_out[:, tile * 128 : (tile + 1) * 128] = tile_of(first, 12 + tile, 4) * token_scale
    for tile in range(7):
        block = tile_of(first, tile, 4) * voxel_scale
        for kind in range(4):
            piece = block[kind * 4 : kind * 4 + 4]
            if kind < 3:
                conv_out[kind * 9 + tile] = piece
            elif tile < 6:
                conv_out[(tile % 3) * 9 + 7 + tile // 3] = piece


def body(hidden_states, attn_gain, qkv_weight, out_weight, up_weight, conv_weight, cotangent):
    vmem = pl.BlockSpec(memory_space=pltpu.VMEM)
    hbm = pl.BlockSpec(memory_space=pl.ANY)
    scratch = [
        pltpu.VMEM((8, 2, 16, E), BF),
        pltpu.VMEM((8, 2, 16, E), BF),
        pltpu.VMEM((8, 2, 4, 16, C), BF),
        pltpu.VMEM((E, 3 * E), BF),
        pltpu.VMEM((E, E), BF),
        pltpu.VMEM((E, E), BF),
        pltpu.VMEM((27, C, C), BF),
        pltpu.VMEM((9 * C, 3 * C), BF),
        pltpu.VMEM((3 * C, 9 * C), BF),
        pltpu.VMEM((6, 18, 16, C), BF),
        pltpu.VMEM((6, 18, 16, C), BF),
        pltpu.VMEM((1024, 9 * C), BF),
        pltpu.VMEM((1024, E), BF),
        pltpu.VMEM((256, E), BF),
        pltpu.VMEM((256, E), F32),
        pltpu.VMEM((256, E), F32),
        pltpu.VMEM((256, E), BF),
        pltpu.VMEM((256, E), BF),
        pltpu.VMEM((256, E), BF),
        pltpu.VMEM((256, 256), F32),
        pltpu.VMEM((256, E), BF),
        pltpu.VMEM((256, E), BF),
        pltpu.VMEM((256, E), F32),
        pltpu.VMEM((256, E), BF),
        pltpu.VMEM((256, E), F32),
        pltpu.VMEM((256, 3 * E), BF),
        pltpu.VMEM((8, 2, 4, 16, C), BF),
        pltpu.VMEM((8, 2, 4, 16, C), BF),
        pltpu.VMEM((8, 2, 16, E), BF),
        pltpu.VMEM((8, 2, 16, E), BF),
        pltpu.SemaphoreType.DMA((4,)),
        pltpu.SemaphoreType.DMA((4, 7)),
        pltpu.SemaphoreType.DMA((4, 7)),
        pltpu.SemaphoreType.DMA((2, 8)),
        pltpu.SemaphoreType.DMA((2, 8)),
    ]
    arrived = (
        jax.ShapeDtypeStruct((8, 2, 4, 16, C), BF),
        jax.ShapeDtypeStruct((8, 2, 16, E), BF),
        jax.ShapeDtypeStruct((8, 16, 256), BF),
        jax.ShapeDtypeStruct((8, 16, 256), BF),
    )
    results = pl.pallas_call(
        block_kernel,
        out_shape=arrived,
        in_specs=[vmem, vmem, hbm, hbm, hbm, hbm, vmem],
        out_specs=[vmem] * 4,
        scratch_shapes=scratch + reducer_scratch(WA) + reducer_scratch(WB),
        compiler_params=pltpu.CompilerParams(
            collective_id=0, has_side_effects=True, vmem_limit_bytes=56 * 2**20
        ),
    )(
        hidden_states,
        attn_gain.reshape(1, E),
        qkv_weight,
        out_weight,
        up_weight,
        conv_weight.reshape(27, C, C),
        cotangent,
    )
    decoded, states, qkv, out, up, conv = pl.pallas_call(
        finish_kernel,
        out_shape=(
            jax.ShapeDtypeStruct(cotangent.shape, BF),
            jax.ShapeDtypeStruct(hidden_states.shape, BF),
        )
        + SHARES,
        in_specs=[vmem] * 4,
        out_specs=[vmem] * 6,
    )(*results)
    return (decoded, states, qkv, out, up, conv.reshape(3, 3, 3, 4, C))


def solution(mesh):
    placed = (P("tm", "height", None, None), P(), P(), P(), P(), P(), P("tm", "height", None, None))
    return jax.shard_map(
        body,
        mesh=mesh,
        in_specs=placed,
        out_specs=(
            P("tm", "height", None, None),
            P("tm", "height", None, None),
            P("height", None),
            P("height", None),
            P("height", None),
            P(None, None, None, "height", None),
        ),
        check_vma=False,
    )
```

```python
import jax
import jax.numpy as jnp
from jax import lax
from jax.experimental import pallas as pl
from jax.experimental.pallas import tpu as pltpu
from jax.sharding import PartitionSpec as P

E = 512
C = 128
EPS = 1e-06
ROOT = 1.0 / 512.0**0.5

MESH = pl.DeviceIdType.MESH
BF = jnp.bfloat16
F32 = jnp.float32


def place():
    t = lax.axis_index("tm")
    h = lax.axis_index("height")
    return t, h, lax.rem(h, 2), lax.rem(h // 2, 4), h // 8


def signal_peers(t, h):
    barrier = pltpu.get_barrier_semaphore()
    c, x, z = lax.rem(h, 2), lax.rem(h // 2, 4), h // 8
    y, far = lax.rem(t, 4), t // 4
    peers = [(lax.rem(t + k, 8), h) for k in range(1, 8)]
    peers += [(t, h + 1 - 2 * c)]
    peers += [(t, z * 8 + lax.rem(x + k, 4) * 2 + c) for k in range(1, 4)]
    for k in range(1, 8):
        to = lax.rem(far * 4 + z + k, 8)
        peers += [(to // 4 * 4 + y, lax.rem(to, 4) * 8 + x * 2 + c)]
    peers += [(lax.rem(t + i, 8), lax.rem(h + j, 32)) for i in (7, 0, 1) for j in (31, 1)]
    for peer in peers:
        pl.semaphore_signal(barrier, inc=1, device_id=peer, device_id_type=MESH)
    return len(peers)


def remote(src, dst, send, recv, peer):
    return pltpu.make_async_remote_copy(
        src_ref=src, dst_ref=dst, send_sem=send, recv_sem=recv, device_id=peer, device_id_type=MESH
    )


class Reducer:
    def __init__(self, refs, where):
        self.grads, self.r1, self.r2x, self.r2y, self.s2x, self.s2y, self.r3x, self.r3y = refs[:8]
        self.s3, self.r4, self.total, self.send, self.recv = refs[8:]
        self.t, self.h, self.c, self.x, self.z = where
        self.y, self.far = lax.rem(self.t, 4), self.t // 4
        self.wide = self.grads.shape[-1] // 4
        self.copies = []

    def start(self, index, src, dst, peer):
        copy = remote(src, dst, self.send.at[index], self.recv.at[index], peer)
        copy.start()
        self.copies.append(copy)

    def wait(self):
        for copy in self.copies:
            copy.wait()
        self.copies = []

    def x_peer(self, to):
        return (self.t, self.z * 8 + to * 2 + self.c)

    def y_peer(self, to):
        return (self.far * 4 + to, self.h)

    def start_core(self):
        c = self.c
        self.start(0, self.grads.at[:, :, 1 - c], self.r1, (self.t, self.h + 1 - 2 * c))

    def start_first(self):
        self.wait()
        c, wide = self.c, self.wide

        def add(i, carry):
            a, b = i // 4, lax.rem(i, 4)
            both = self.grads[a, b, c].astype(F32) + self.r1[a, b].astype(F32)
            self.grads[a, b, c] = both.astype(BF)
            return carry

        lax.fori_loop(0, 16, add, 0)
        for k in range(1, 4):
            to = lax.rem(self.x + k, 4)
            self.start(k, self.grads.at[pl.ds(0, 2), to, c], self.r2x.at[k - 1], self.x_peer(to))
            to = lax.rem(self.y + k, 4)
            columns = pl.ds(pl.multiple_of(to * wide, 128), wide)
            self.start(3 + k, self.grads.at[pl.ds(2, 2), :, c, :, columns], self.r2y.at[k - 1], self.y_peer(to))

    def start_second(self):
        self.wait()
        c, wide = self.c, self.wide
        for i in range(2):
            both = self.grads[i, self.x, c].astype(F32)
            for k in range(3):
                both = both + self.r2x[k, i].astype(F32)
            both = both.astype(BF)
            for q in range(4):
                self.s2x[q, i] = both[:, q * wide : (q + 1) * wide]
        columns = pl.ds(pl.multiple_of(self.y * wide, 128), wide)
        for i in range(2):
            for q in range(4):
                both = self.grads[2 + i, q, c, :, columns].astype(F32)
                for k in range(3):
                    both = both + self.r2y[k, i, q].astype(F32)
                self.s2y[q, i] = both.astype(BF)
        for k in range(1, 4):
            to = lax.rem(self.y + k, 4)
            self.start(6 + k, self.s2x.at[to], self.r3x.at[k - 1], self.y_peer(to))
            to = lax.rem(self.x + k, 4)
            self.start(9 + k, self.s2y.at[to], self.r3y.at[k - 1], self.x_peer(to))

    def start_rows(self):
        self.wait()
        for i in range(4):
            mine, parts = (self.s2x[self.y, i], self.r3x) if i < 2 else (self.s2y[self.x, i - 2], self.r3y)
            both = mine.astype(F32)
            for k in range(3):
                both = both + parts[k, i % 2].astype(F32)
            self.s3[i] = both.astype(BF)
        for k in range(1, 8):
            to = lax.rem(self.far * 4 + self.z + k, 8)
            far, z = to // 4, lax.rem(to, 4)
            peer = (far * 4 + self.y, z * 8 + self.x * 2 + self.c)
            self.start(12 + k, self.s3.at[z], self.r4.at[k - 1], peer)

    def start_gather(self):
        self.wait()
        both = self.s3[self.z].astype(F32)
        for k in range(7):
            both = both + self.r4[k].astype(F32)
        self.total[self.y] = both.astype(BF)
        for k in range(1, 4):
            to = lax.rem(self.y + k, 4)
            self.start(19 + k, self.total.at[self.y], self.total.at[self.y], self.y_peer(to))


def reducer_scratch(width):
    wide = width // 4
    return [
        pltpu.VMEM((4, 4, 2, 16, width), BF),
        pltpu.VMEM((4, 4, 16, width), BF),
        pltpu.VMEM((3, 2, 16, width), BF),
        pltpu.VMEM((3, 2, 4, 16, wide), BF),
        pltpu.VMEM((4, 2, 16, wide), BF),
        pltpu.VMEM((4, 2, 16, wide), BF),
        pltpu.VMEM((3, 2, 16, wide), BF),
        pltpu.VMEM((3, 2, 16, wide), BF),
        pltpu.VMEM((4, 16, wide), BF),
        pltpu.VMEM((7, 16, wide), BF),
        pltpu.VMEM((4, 16, wide), BF),
        pltpu.SemaphoreType.DMA((23,)),
        pltpu.SemaphoreType.DMA((23,)),
    ]


def nn(a, b):
    return jnp.dot(a, b, preferred_element_type=F32)


def nt(a, b):
    return lax.dot_general(a, b, (((1,), (1,)), ((), ())), preferred_element_type=F32)


def tn(a, b):
    return lax.dot_general(a, b, (((0,), (0,)), ((), ())), preferred_element_type=F32)


def iota(shape, dim):
    return lax.broadcasted_iota(jnp.int32, shape, dim)


def ones_where(cond):
    return jnp.where(cond, 1.0, 0.0).astype(BF)


def swap_matrix():
    r, s = iota((256, 256), 0), iota((256, 256), 1)
    return ones_where(s == (r & 15) * 16 + (r >> 4))


def to_blocks_matrix():
    r, s = iota((128, 128), 0), iota((128, 128), 1)
    return ones_where(s == ((r >> 3) & 1) * 64 + (r >> 4) * 8 + (r & 7))


def from_blocks_matrix():
    r, s = iota((128, 128), 0), iota((128, 128), 1)
    return ones_where(s == ((r >> 3) & 7) * 16 + (r >> 6) * 8 + (r & 7))


def spread_matrix():
    r, s = iota((384, 512), 0), iota((384, 512), 1)
    channel = r & 127
    return ones_where(s == (channel >> 2) * 16 + (r >> 7) * 4 + (channel & 3))


def move(matrix, rows):
    return nn(matrix, rows).astype(BF)


def rms_scale(rows):
    return lax.rsqrt(jnp.mean(rows * rows, axis=-1, keepdims=True) + EPS)


def norm_back(rows, upstream):
    factor = rms_scale(rows)
    unit = rows * factor
    return factor * (upstream - unit * jnp.mean(upstream * unit, axis=-1, keepdims=True))


def later_frames(rows, by):
    count = rows.shape[0]
    frame = iota(rows.shape, 0) & 15
    return jnp.where(frame + by <= 15, pltpu.roll(rows, count - by, 0), 0.0)


def earlier_frames(rows, by):
    frame = iota(rows.shape, 0) & 15
    return jnp.where(frame >= by, pltpu.roll(rows, by, 0), 0.0)


def move_lanes(rows, matrix):
    return nn(rows, matrix).astype(BF)


class Halo:
    def __init__(self, cells, send, recv, t, h):
        self.cells, self.t, self.h = cells, t, h
        inner = {-1: (pl.ds(1, 1), pl.ds(1, 1)), 0: (pl.ds(1, 4), pl.ds(1, 16)), 1: (pl.ds(4, 1), pl.ds(16, 1))}
        outer = {-1: (pl.ds(5, 1), pl.ds(17, 1)), 0: (pl.ds(1, 4), pl.ds(1, 16)), 1: (pl.ds(0, 1), pl.ds(0, 1))}
        self.copies = []
        for i in (-1, 0, 1):
            for j in (-1, 0, 1):
                if i or j:
                    at = len(self.copies)
                    peer = (lax.rem(t + 8 + j, 8), lax.rem(h + 32 + i, 32))
                    src = cells.at[inner[i][0], inner[j][1]]
                    dst = cells.at[outer[i][0], outer[j][1]]
                    self.copies.append(remote(src, dst, send.at[at], recv.at[at], peer))

    def start(self):
        for copy in self.copies:
            copy.start()

    def finish(self):
        for copy in self.copies:
            copy.wait()
        side, edge = jnp.zeros((6, 16, C), BF), jnp.zeros((18, 16, C), BF)

        @pl.when(self.t == 0)
        def _():
            self.cells[:, 0] = side

        @pl.when(self.t == 7)
        def _():
            self.cells[:, 17] = side

        @pl.when(self.h == 0)
        def _():
            self.cells[0] = edge

        @pl.when(self.h == 31)
        def _():
            self.cells[5] = edge


def block_kernel(
    hs_hbm, gain_in, wqkv_in, wout_in, wup_in, wconv_in, cot_in,
    dec_out, states_out, conv_out, rest_out, qk_out,
    hs_in, hs_send, hs_recv, cot_recv, wqkv, wout, wup, wconv, wf, wb,
    cot, pix, xc, shifted, normed, q_raw, k_raw, query, keys, values, probs, mixed, merged, pre,
    grad_pre, grad_merged, grad_joined, dec_send, dec_recv, gs_send, gs_recv,
    load_sem, a2a_send, a2a_recv, halo_send, halo_recv,
    *reducers,
):
    t, h, c, x, z = place()
    expected = signal_peers(t, h)
    conv, rest, qk = (Reducer(reducers[13 * i : 13 * i + 13], (t, h, c, x, z)) for i in range(3))
    loads = [
        pltpu.make_async_copy(src, dst, load_sem.at[i])
        for i, (src, dst) in enumerate(
            (
                (hs_hbm, hs_in),
                (cot_in.at[:, :, pl.ds(pl.multiple_of(t * 16, 16), 16), :], cot_recv.at[t]),
                (wconv_in, wconv),
                (wqkv_in, wqkv),
                (wout_in, wout),
                (wup_in, wup),
            )
        )
    ]
    for load in loads:
        load.start()
    swap = swap_matrix()
    to_blocks = to_blocks_matrix()
    loads[0].wait()
    for f in range(2):
        moved = move(to_blocks, hs_in[f].reshape(128, E))
        hs_send[:, f] = moved.reshape(8, 16, E)
    pl.semaphore_wait(pltpu.get_barrier_semaphore(), expected)

    def exchange(kind, src_of, dst):
        copies = []
        for k in range(1, 8):
            to = lax.rem(t + k, 8)
            copy = remote(src_of(to), dst.at[t], a2a_send.at[kind, k - 1], a2a_recv.at[kind, k - 1], (to, h))
            copy.start()
            copies.append(copy)
        return copies

    hs_copies = exchange(0, lambda to: hs_send.at[to], hs_recv)
    cot_copies = exchange(
        1, lambda to: cot_in.at[:, :, pl.ds(pl.multiple_of(to * 16, 16), 16), :], cot_recv
    )
    hs_recv[t] = hs_send[t]
    cot_halo = Halo(cot, halo_send.at[0], halo_recv.at[0], t, h)
    pix_halo = Halo(pix, halo_send.at[1], halo_recv.at[1], t, h)

    loads[1].wait()
    loads[2].wait()
    for a in range(3):
        for k in range(9):
            tap = wconv[a * 9 + k]
            wf[k * C : (k + 1) * C, a * C : (a + 1) * C] = tap
            wb[a * C : (a + 1) * C, k * C : (k + 1) * C] = tap
    for load in loads[3:]:
        load.wait()

    for copy in hs_copies:
        copy.wait()
    tokens = move(swap, hs_recv[...].reshape(256, E))
    hs_send[...] = tokens.reshape(8, 2, 16, E)
    wide = tokens.astype(F32)
    normed[...] = (wide * rms_scale(wide) * gain_in[...]).astype(BF)
    q_raw[...] = nn(normed[...], wqkv[:, :E])
    k_raw[...] = nn(normed[...], wqkv[:, E : 2 * E])
    values[...] = nn(normed[...], wqkv[:, 2 * E :]).astype(BF)
    raw = q_raw[...]
    query[...] = (raw * rms_scale(raw)).astype(BF)
    raw = k_raw[...]
    keys[...] = (raw * rms_scale(raw)).astype(BF)

    for copy in cot_copies:
        copy.wait()
    for r in range(4):
        cells = move(swap, cot_recv[:, :, r].reshape(256, C))
        cot[r + 1, 1:17] = cells.reshape(16, 16, C)
    cot_halo.start()

    rows, cols = iota((256, 256), 0), iota((256, 256), 1)
    allowed = ((rows >> 4) == (cols >> 4)) & (cols <= rows)
    weights = jnp.where(allowed, jnp.exp(nt(query[...], keys[...]) * ROOT), 0.0)
    probs[...] = weights / jnp.sum(weights, axis=-1, keepdims=True)
    mixed[...] = nn(probs[...].astype(BF), values[...]).astype(BF)

    tokens_wide = hs_send[...].reshape(256, E).astype(F32)
    merged[...] = (tokens_wide + nn(mixed[...], wout[...])).astype(BF)
    pre[...] = nn(merged[...], wup[...])
    act = pre[...]
    act = (act / (1.0 + jnp.exp(-act))).astype(BF)
    for i in range(2):
        for a in range(2):
            for j in range(8):
                for b in range(2):
                    at = (i * 8 + j) * 16
                    kind = (2 * a + b) * C
                    pix[2 * i + a + 1, 2 * j + b + 1] = act[at : at + 16, kind : kind + C]
    pix_halo.start()

    spread = spread_matrix()
    for r in range(4):
        cells = pix[r + 1, 1:17].reshape(256, C).astype(F32)
        taps = [earlier_frames(cells, 2).astype(BF), earlier_frames(cells, 1).astype(BF), cells.astype(BF)]
        shifted[r * 256 : (r + 1) * 256] = move_lanes(jnp.concatenate(taps, axis=1), spread)
    cot_halo.finish()
    for r in range(4):
        for b in range(3):
            for k in range(3):
                at = (b * 3 + k) * C
                xc[r * 256 : (r + 1) * 256, at : at + C] = cot[r + 2 - b, 2 - k : 18 - k].reshape(256, C)
    quarter = (iota((512, C), 0) >> 2) & 3
    extra = [tn(shifted[...], xc[:, k * C : (k + 1) * C]) for k in (7, 8)]
    for tile in range(7):
        total = tn(shifted[...], xc[:, tile * C : (tile + 1) * C])
        if tile < 6:
            total = jnp.where(quarter == 3, pltpu.roll(extra[tile // 3], 12 - 4 * (tile % 3), 0), total)
        conv.grads[:, :, :, :, tile * C : (tile + 1) * C] = total.astype(BF).reshape(4, 4, 2, 16, C)
    conv.grads[:, :, :, :, 7 * C :] = jnp.zeros((4, 4, 2, 16, C), BF)
    conv.start_core()
    for r in range(4):
        terms = nt(xc[r * 256 : (r + 1) * 256], wb[...])
        grad = terms[:, 2 * C :] + later_frames(terms[:, C : 2 * C], 1) + later_frames(terms[:, :C], 2)
        i, a = r // 2, r % 2
        for j in range(8):
            at = (i * 8 + j) * 16
            pre_pair = pre[at : at + 16, 2 * a * C : (2 * a + 2) * C]
            gate = 1.0 / (1.0 + jnp.exp(-pre_pair))
            slope = gate * (1.0 + pre_pair * (1.0 - gate))
            pair = jnp.concatenate([grad[2 * j * 16 : 2 * j * 16 + 16], grad[2 * j * 16 + 16 : 2 * j * 16 + 32]], axis=1)
            grad_pre[at : at + 16, 2 * a * C : (2 * a + 2) * C] = (pair * slope).astype(BF)
    conv.start_first()

    grad_merged[...] = nt(grad_pre[...], wup[...])
    low = grad_merged[...].astype(BF)
    grad_mixed = nt(low, wout[...]).astype(BF)
    grad_joined[:, 2 * E :] = tn(probs[...].astype(BF), grad_mixed).astype(BF)
    rest.grads[:, :, :, :, :E] = tn(merged[...], grad_pre[...]).astype(BF).reshape(4, 4, 2, 16, E)
    rest.grads[:, :, :, :, E : 2 * E] = tn(mixed[...], low).astype(BF).reshape(4, 4, 2, 16, E)
    rest.grads[:, :, :, :, 2 * E :] = tn(normed[...], grad_joined[:, 2 * E :]).astype(BF).reshape(4, 4, 2, 16, E)
    rest.start_core()

    grad_probs = nt(grad_mixed, values[...])
    inner = jnp.sum(probs[...] * grad_probs, axis=-1, keepdims=True)
    grad_scores = (probs[...] * (grad_probs - inner) * ROOT).astype(BF)
    grad_joined[:, :E] = norm_back(q_raw[...], nn(grad_scores, keys[...])).astype(BF)
    grad_joined[:, E : 2 * E] = norm_back(k_raw[...], tn(grad_scores, query[...])).astype(BF)
    rest.start_first()
    for part in range(2):
        at = part * E
        block = tn(normed[...], grad_joined[:, at : at + E])
        qk.grads[:, :, :, :, at : at + E] = block.astype(BF).reshape(4, 4, 2, 16, E)
    qk.start_core()

    grad_normed = nt(grad_joined[...], wqkv[...])
    states = norm_back(hs_send[...].reshape(256, E).astype(F32), grad_normed * gain_in[...])
    states = (grad_merged[...] + states).astype(BF)
    gs_send[...] = move(swap, states).reshape(8, 2, 16, E)
    qk.start_first()
    gs_copies = exchange(2, lambda to: gs_send.at[to], gs_recv)
    gs_recv[t] = gs_send[t]
    conv.start_second()

    pix_halo.finish()
    for r in range(4):
        taps = [pix[r + b, k : k + 16].reshape(256, C) for b in range(3) for k in range(3)]
        terms = nn(jnp.concatenate(taps, axis=1), wf[...])
        cells = terms[:, 2 * C :] + earlier_frames(terms[:, C : 2 * C], 1) + earlier_frames(terms[:, :C], 2)
        dec_send[:, :, r] = move(swap, cells.astype(BF)).reshape(8, 2, 16, C)
    dec_copies = exchange(3, lambda to: dec_send.at[to], dec_recv)
    dec_recv[t] = dec_send[t]

    rest.start_second()
    conv.start_rows()
    qk.start_second()
    rest.start_rows()
    qk.start_rows()
    conv.start_gather()
    rest.start_gather()
    qk.start_gather()
    for copy in gs_copies:
        copy.wait()
    states_out[...] = gs_recv[...]
    for copy in dec_copies:
        copy.wait()
    dec_out[...] = dec_recv[...]
    conv.wait()
    rest.wait()
    conv_out[...] = conv.total[...]
    rest_out[...] = rest.total[...]
    qk.wait()
    qk_out[...] = qk.total[...]


WIDTHS = (1024, 1536, 1024)
SHARES = (
    jax.ShapeDtypeStruct((16, 1536), F32),
    jax.ShapeDtypeStruct((16, 512), F32),
    jax.ShapeDtypeStruct((16, 512), F32),
    jax.ShapeDtypeStruct((27, 4, 128), F32),
)


def finish_kernel(dec, states, conv_sum, rest_sum, qk_sum, decoded_out, states_out, qkv_out, out_out, up_out, conv_out):
    token_scale = 1.0 / 65536.0**0.5
    voxel_scale = 1.0 / 262144.0**0.5
    from_blocks = from_blocks_matrix()
    for f in range(2):
        states_out[f] = move(from_blocks, states[:, f].reshape(128, E)).reshape(2, 64, E)
    for k in range(8):
        decoded_out[:, :, k * 16 : (k + 1) * 16, :] = dec[k]

    def tile_of(total, tile):
        count = total.shape[2] // 128
        at = (tile % count) * 128
        return total[tile // count][:, at : at + 128].astype(F32)

    for tile in range(8):
        qkv_out[:, tile * 128 : (tile + 1) * 128] = tile_of(qk_sum, tile) * token_scale
    for tile in range(4):
        up_out[:, tile * 128 : (tile + 1) * 128] = tile_of(rest_sum, tile) * token_scale
        out_out[:, tile * 128 : (tile + 1) * 128] = tile_of(rest_sum, 4 + tile) * token_scale
        qkv_out[:, 2 * E + tile * 128 : 2 * E + (tile + 1) * 128] = tile_of(rest_sum, 8 + tile) * token_scale
    for tile in range(7):
        block = tile_of(conv_sum, tile) * voxel_scale
        for kind in range(4):
            piece = block[kind * 4 : kind * 4 + 4]
            if kind < 3:
                conv_out[kind * 9 + tile] = piece
            elif tile < 6:
                conv_out[(tile % 3) * 9 + 7 + tile // 3] = piece


def body(hidden_states, attn_gain, qkv_weight, out_weight, up_weight, conv_weight, cotangent):
    vmem = pl.BlockSpec(memory_space=pltpu.VMEM)
    hbm = pl.BlockSpec(memory_space=pl.ANY)
    scratch = [
        pltpu.VMEM((2, 2, 64, E), BF),
        pltpu.VMEM((8, 2, 16, E), BF),
        pltpu.VMEM((8, 2, 16, E), BF),
        pltpu.VMEM((8, 2, 4, 16, C), BF),
        pltpu.VMEM((E, 3 * E), BF),
        pltpu.VMEM((E, E), BF),
        pltpu.VMEM((E, E), BF),
        pltpu.VMEM((27, C, C), BF),
        pltpu.VMEM((9 * C, 3 * C), BF),
        pltpu.VMEM((3 * C, 9 * C), BF),
        pltpu.VMEM((6, 18, 16, C), BF),
        pltpu.VMEM((6, 18, 16, C), BF),
        pltpu.VMEM((1024, 9 * C), BF),
        pltpu.VMEM((1024, E), BF),
        pltpu.VMEM((256, E), BF),
        pltpu.VMEM((256, E), F32),
        pltpu.VMEM((256, E), F32),
        pltpu.VMEM((256, E), BF),
        pltpu.VMEM((256, E), BF),
        pltpu.VMEM((256, E), BF),
        pltpu.VMEM((256, 256), F32),
        pltpu.VMEM((256, E), BF),
        pltpu.VMEM((256, E), BF),
        pltpu.VMEM((256, E), F32),
        pltpu.VMEM((256, E), BF),
        pltpu.VMEM((256, E), F32),
        pltpu.VMEM((256, 3 * E), BF),
        pltpu.VMEM((8, 2, 4, 16, C), BF),
        pltpu.VMEM((8, 2, 4, 16, C), BF),
        pltpu.VMEM((8, 2, 16, E), BF),
        pltpu.VMEM((8, 2, 16, E), BF),
        pltpu.SemaphoreType.DMA((6,)),
        pltpu.SemaphoreType.DMA((4, 7)),
        pltpu.SemaphoreType.DMA((4, 7)),
        pltpu.SemaphoreType.DMA((2, 8)),
        pltpu.SemaphoreType.DMA((2, 8)),
    ]
    arrived = (
        jax.ShapeDtypeStruct((8, 2, 4, 16, C), BF),
        jax.ShapeDtypeStruct((8, 2, 16, E), BF),
    ) + tuple(jax.ShapeDtypeStruct((4, 16, width // 4), BF) for width in WIDTHS)
    results = pl.pallas_call(
        block_kernel,
        out_shape=arrived,
        in_specs=[hbm, vmem, hbm, hbm, hbm, hbm, hbm],
        out_specs=[vmem] * 5,
        scratch_shapes=scratch + [buffer for width in WIDTHS for buffer in reducer_scratch(width)],
        compiler_params=pltpu.CompilerParams(
            collective_id=0, has_side_effects=True, vmem_limit_bytes=56 * 2**20
        ),
    )(
        hidden_states,
        attn_gain.reshape(1, E),
        qkv_weight,
        out_weight,
        up_weight,
        conv_weight.reshape(27, C, C),
        cotangent,
    )
    decoded, states, qkv, out, up, conv = pl.pallas_call(
        finish_kernel,
        out_shape=(
            jax.ShapeDtypeStruct(cotangent.shape, BF),
            jax.ShapeDtypeStruct(hidden_states.shape, BF),
        )
        + SHARES,
        in_specs=[vmem] * 5,
        out_specs=[vmem] * 6,
    )(*results)
    return (decoded, states, qkv, out, up, conv.reshape(3, 3, 3, 4, C))


def solution(mesh):
    placed = (P("tm", "height", None, None), P(), P(), P(), P(), P(), P("tm", "height", None, None))
    return jax.shard_map(
        body,
        mesh=mesh,
        in_specs=placed,
        out_specs=(
            P("tm", "height", None, None),
            P("tm", "height", None, None),
            P("height", None),
            P("height", None),
            P("height", None),
            P(None, None, None, "height", None),
        ),
        check_vma=False,
    )
```

```python
import jax
import jax.numpy as jnp
from jax import lax
from jax.experimental import pallas as pl
from jax.experimental.pallas import tpu as pltpu
from jax.sharding import PartitionSpec as P

E = 512
C = 128
EPS = 1e-06
ROOT = 1.0 / 512.0**0.5

MESH = pl.DeviceIdType.MESH
BF = jnp.bfloat16
F32 = jnp.float32


def place():
    t = lax.axis_index("tm")
    h = lax.axis_index("height")
    return t, h, lax.rem(h, 2), lax.rem(h // 2, 4), h // 8


def signal_peers(t, h):
    barrier = pltpu.get_barrier_semaphore()
    c, x, z = lax.rem(h, 2), lax.rem(h // 2, 4), h // 8
    y, far = lax.rem(t, 4), t // 4
    peers = [(lax.rem(t + k, 8), h) for k in range(1, 8)]
    peers += [(t, h + 1 - 2 * c)]
    peers += [(t, z * 8 + lax.rem(x + k, 4) * 2 + c) for k in range(1, 4)]
    for k in range(1, 8):
        to = lax.rem(far * 4 + z + k, 8)
        peers += [(to // 4 * 4 + y, lax.rem(to, 4) * 8 + x * 2 + c)]
    peers += [(lax.rem(t + i, 8), lax.rem(h + j, 32)) for i in (7, 0, 1) for j in (31, 1)]
    for peer in peers:
        pl.semaphore_signal(barrier, inc=1, device_id=peer, device_id_type=MESH)
    return len(peers)


def remote(src, dst, send, recv, peer):
    return pltpu.make_async_remote_copy(
        src_ref=src, dst_ref=dst, send_sem=send, recv_sem=recv, device_id=peer, device_id_type=MESH
    )


class Reducer:
    def __init__(self, refs, where):
        self.grads, self.r1, self.r2x, self.r2y, self.s2x, self.s2y, self.r3x, self.r3y = refs[:8]
        self.s3, self.r4, self.total, self.send, self.recv = refs[8:]
        self.t, self.h, self.c, self.x, self.z = where
        self.y, self.far = lax.rem(self.t, 4), self.t // 4
        self.wide = self.grads.shape[-1] // 4
        self.by_x = self.s2x.shape[1]
        self.copies = []

    def start(self, index, src, dst, peer):
        copy = remote(src, dst, self.send.at[index], self.recv.at[index], peer)
        copy.start()
        self.copies.append(copy)

    def wait(self):
        for copy in self.copies:
            copy.wait()
        self.copies = []

    def x_peer(self, to):
        return (self.t, self.z * 8 + to * 2 + self.c)

    def y_peer(self, to):
        return (self.far * 4 + to, self.h)

    def start_core(self):
        c = self.c
        self.start(0, self.grads.at[:, :, 1 - c], self.r1, (self.t, self.h + 1 - 2 * c))

    def start_first(self):
        self.wait()
        c, wide = self.c, self.wide

        def add(i, carry):
            a, b = i // 4, lax.rem(i, 4)
            both = self.grads[a, b, c].astype(F32) + self.r1[a, b].astype(F32)
            self.grads[a, b, c] = both.astype(BF)
            return carry

        lax.fori_loop(0, 16, add, 0)
        for k in range(1, 4):
            to = lax.rem(self.x + k, 4)
            self.start(k, self.grads.at[pl.ds(0, self.by_x), to, c], self.r2x.at[k - 1], self.x_peer(to))
            to = lax.rem(self.y + k, 4)
            columns = pl.ds(pl.multiple_of(to * wide, 128), wide)
            self.start(3 + k, self.grads.at[pl.ds(self.by_x, 4 - self.by_x), :, c, :, columns], self.r2y.at[k - 1], self.y_peer(to))

    def start_second(self):
        self.wait()
        c, wide = self.c, self.wide
        for i in range(self.by_x):
            both = self.grads[i, self.x, c].astype(F32)
            for k in range(3):
                both = both + self.r2x[k, i].astype(F32)
            both = both.astype(BF)
            for q in range(4):
                self.s2x[q, i] = both[:, q * wide : (q + 1) * wide]
        columns = pl.ds(pl.multiple_of(self.y * wide, 128), wide)
        for i in range(4 - self.by_x):
            for q in range(4):
                both = self.grads[self.by_x + i, q, c, :, columns].astype(F32)
                for k in range(3):
                    both = both + self.r2y[k, i, q].astype(F32)
                self.s2y[q, i] = both.astype(BF)
        for k in range(1, 4):
            to = lax.rem(self.y + k, 4)
            self.start(6 + k, self.s2x.at[to], self.r3x.at[k - 1], self.y_peer(to))
            to = lax.rem(self.x + k, 4)
            self.start(9 + k, self.s2y.at[to], self.r3y.at[k - 1], self.x_peer(to))

    def start_rows(self):
        self.wait()
        for i in range(4):
            parts, at = (self.r3x, i) if i < self.by_x else (self.r3y, i - self.by_x)
            both = (self.s2x[self.y, at] if i < self.by_x else self.s2y[self.x, at]).astype(F32)
            for k in range(3):
                both = both + parts[k, at].astype(F32)
            self.s3[i] = both.astype(BF)
        for k in range(1, 8):
            to = lax.rem(self.far * 4 + self.z + k, 8)
            far, z = to // 4, lax.rem(to, 4)
            peer = (far * 4 + self.y, z * 8 + self.x * 2 + self.c)
            self.start(12 + k, self.s3.at[z], self.r4.at[k - 1], peer)

    def start_gather(self):
        self.wait()
        both = self.s3[self.z].astype(F32)
        for k in range(7):
            both = both + self.r4[k].astype(F32)
        self.total[self.y] = both.astype(BF)
        for k in range(1, 4):
            to = lax.rem(self.y + k, 4)
            self.start(19 + k, self.total.at[self.y], self.total.at[self.y], self.y_peer(to))


def reducer_scratch(width, by_x):
    wide, by_y = width // 4, 4 - by_x
    return [
        pltpu.VMEM((4, 4, 2, 16, width), BF),
        pltpu.VMEM((4, 4, 16, width), BF),
        pltpu.VMEM((3, by_x, 16, width), BF),
        pltpu.VMEM((3, by_y, 4, 16, wide), BF),
        pltpu.VMEM((4, by_x, 16, wide), BF),
        pltpu.VMEM((4, by_y, 16, wide), BF),
        pltpu.VMEM((3, by_x, 16, wide), BF),
        pltpu.VMEM((3, by_y, 16, wide), BF),
        pltpu.VMEM((4, 16, wide), BF),
        pltpu.VMEM((7, 16, wide), BF),
        pltpu.VMEM((4, 16, wide), BF),
        pltpu.SemaphoreType.DMA((23,)),
        pltpu.SemaphoreType.DMA((23,)),
    ]


def nn(a, b):
    return jnp.dot(a, b, preferred_element_type=F32)


def nt(a, b):
    return lax.dot_general(a, b, (((1,), (1,)), ((), ())), preferred_element_type=F32)


def tn(a, b):
    return lax.dot_general(a, b, (((0,), (0,)), ((), ())), preferred_element_type=F32)


def iota(shape, dim):
    return lax.broadcasted_iota(jnp.int32, shape, dim)


def ones_where(cond):
    return jnp.where(cond, 1.0, 0.0).astype(BF)


def swap_matrix():
    r, s = iota((256, 256), 0), iota((256, 256), 1)
    return ones_where(s == (r & 15) * 16 + (r >> 4))


def to_blocks_matrix():
    r, s = iota((128, 128), 0), iota((128, 128), 1)
    return ones_where(s == ((r >> 3) & 1) * 64 + (r >> 4) * 8 + (r & 7))


def from_blocks_matrix():
    r, s = iota((128, 128), 0), iota((128, 128), 1)
    return ones_where(s == ((r >> 3) & 7) * 16 + (r >> 6) * 8 + (r & 7))


def spread_matrix():
    r, s = iota((384, 512), 0), iota((384, 512), 1)
    channel = r & 127
    return ones_where(s == (channel >> 2) * 16 + (r >> 7) * 4 + (channel & 3))


def move(matrix, rows):
    return nn(matrix, rows).astype(BF)


def rms_scale(rows):
    return lax.rsqrt(jnp.mean(rows * rows, axis=-1, keepdims=True) + EPS)


def norm_back(rows, upstream):
    factor = rms_scale(rows)
    unit = rows * factor
    return factor * (upstream - unit * jnp.mean(upstream * unit, axis=-1, keepdims=True))


def later_frames(rows, by):
    count = rows.shape[0]
    frame = iota(rows.shape, 0) & 15
    return jnp.where(frame + by <= 15, pltpu.roll(rows, count - by, 0), 0.0)


def earlier_frames(rows, by):
    frame = iota(rows.shape, 0) & 15
    return jnp.where(frame >= by, pltpu.roll(rows, by, 0), 0.0)


def move_lanes(rows, matrix):
    return nn(rows, matrix).astype(BF)


class Halo:
    def __init__(self, cells, send, recv, t, h):
        self.cells, self.t, self.h = cells, t, h
        inner = {-1: (pl.ds(1, 1), pl.ds(1, 1)), 0: (pl.ds(1, 4), pl.ds(1, 16)), 1: (pl.ds(4, 1), pl.ds(16, 1))}
        outer = {-1: (pl.ds(5, 1), pl.ds(17, 1)), 0: (pl.ds(1, 4), pl.ds(1, 16)), 1: (pl.ds(0, 1), pl.ds(0, 1))}
        self.copies = []
        for i in (-1, 0, 1):
            for j in (-1, 0, 1):
                if i or j:
                    at = len(self.copies)
                    peer = (lax.rem(t + 8 + j, 8), lax.rem(h + 32 + i, 32))
                    src = cells.at[inner[i][0], inner[j][1]]
                    dst = cells.at[outer[i][0], outer[j][1]]
                    self.copies.append(remote(src, dst, send.at[at], recv.at[at], peer))

    def start(self):
        for copy in self.copies:
            copy.start()

    def finish(self):
        for copy in self.copies:
            copy.wait()
        side, edge = jnp.zeros((6, 16, C), BF), jnp.zeros((18, 16, C), BF)

        @pl.when(self.t == 0)
        def _():
            self.cells[:, 0] = side

        @pl.when(self.t == 7)
        def _():
            self.cells[:, 17] = side

        @pl.when(self.h == 0)
        def _():
            self.cells[0] = edge

        @pl.when(self.h == 31)
        def _():
            self.cells[5] = edge


def block_kernel(
    hs_hbm, gain_in, wqkv_in, wout_in, wup_in, wconv_in, cot_in,
    dec_out, states_out, conv_out, rest_out, qk_out,
    hs_in, hs_send, hs_recv, cot_recv, wqkv, wout, wup, wconv, wf, wb,
    cot, pix, xc, shifted, normed, q_raw, k_raw, query, keys, values, probs, mixed, merged, pre,
    grad_pre, grad_merged, grad_joined, dec_send, dec_recv, gs_send, gs_recv,
    load_sem, a2a_send, a2a_recv, halo_send, halo_recv,
    *reducers,
):
    t, h, c, x, z = place()
    expected = signal_peers(t, h)
    conv, rest, qk = (Reducer(reducers[13 * i : 13 * i + 13], (t, h, c, x, z)) for i in range(3))
    loads = [
        pltpu.make_async_copy(src, dst, load_sem.at[i])
        for i, (src, dst) in enumerate(
            (
                (hs_hbm, hs_in),
                (cot_in.at[:, :, pl.ds(pl.multiple_of(t * 16, 16), 16), :], cot_recv.at[t]),
                (wconv_in, wconv),
                (wqkv_in, wqkv),
                (wout_in, wout),
                (wup_in, wup),
            )
        )
    ]
    for load in loads:
        load.start()
    pl.semaphore_wait(pltpu.get_barrier_semaphore(), expected)

    def exchange(kind, src_of, dst):
        copies = []
        for k in (4, 3, 5, 2, 6, 1, 7):
            to = lax.rem(t + k, 8)
            copy = remote(src_of(to), dst.at[t], a2a_send.at[kind, k - 1], a2a_recv.at[kind, k - 1], (to, h))
            copy.start()
            copies.append(copy)
        return copies

    cot_copies = exchange(
        1, lambda to: cot_in.at[:, :, pl.ds(pl.multiple_of(to * 16, 16), 16), :], cot_recv
    )
    swap = swap_matrix()
    to_blocks = to_blocks_matrix()
    loads[0].wait()
    for f in range(2):
        moved = move(to_blocks, hs_in[f].reshape(128, E))
        hs_send[:, f] = moved.reshape(8, 16, E)

    hs_copies = exchange(0, lambda to: hs_send.at[to], hs_recv)
    hs_recv[t] = hs_send[t]
    cot_halo = Halo(cot, halo_send.at[0], halo_recv.at[0], t, h)
    pix_halo = Halo(pix, halo_send.at[1], halo_recv.at[1], t, h)

    loads[1].wait()
    loads[2].wait()
    for a in range(3):
        for k in range(9):
            tap = wconv[a * 9 + k]
            wf[k * C : (k + 1) * C, a * C : (a + 1) * C] = tap
            wb[a * C : (a + 1) * C, k * C : (k + 1) * C] = tap
    for load in loads[3:]:
        load.wait()

    for copy in cot_copies:
        copy.wait()
    for r in range(4):
        cells = move(swap, cot_recv[:, :, r].reshape(256, C))
        cot[r + 1, 1:17] = cells.reshape(16, 16, C)
    cot_halo.start()

    for copy in hs_copies:
        copy.wait()
    tokens = move(swap, hs_recv[...].reshape(256, E))
    hs_send[...] = tokens.reshape(8, 2, 16, E)
    wide = tokens.astype(F32)
    normed[...] = (wide * rms_scale(wide) * gain_in[...]).astype(BF)
    q_raw[...] = nn(normed[...], wqkv[:, :E])
    k_raw[...] = nn(normed[...], wqkv[:, E : 2 * E])
    values[...] = nn(normed[...], wqkv[:, 2 * E :]).astype(BF)
    raw = q_raw[...]
    query[...] = (raw * rms_scale(raw)).astype(BF)
    raw = k_raw[...]
    keys[...] = (raw * rms_scale(raw)).astype(BF)

    rows, cols = iota((256, 256), 0), iota((256, 256), 1)
    allowed = ((rows >> 4) == (cols >> 4)) & (cols <= rows)
    weights = jnp.where(allowed, jnp.exp(nt(query[...], keys[...]) * ROOT), 0.0)
    probs[...] = weights / jnp.sum(weights, axis=-1, keepdims=True)
    mixed[...] = nn(probs[...].astype(BF), values[...]).astype(BF)

    tokens_wide = hs_send[...].reshape(256, E).astype(F32)
    merged[...] = (tokens_wide + nn(mixed[...], wout[...])).astype(BF)
    pre[...] = nn(merged[...], wup[...])
    act = pre[...]
    act = (act / (1.0 + jnp.exp(-act))).astype(BF)
    for i in range(2):
        for a in range(2):
            for j in range(8):
                for b in range(2):
                    at = (i * 8 + j) * 16
                    kind = (2 * a + b) * C
                    pix[2 * i + a + 1, 2 * j + b + 1] = act[at : at + 16, kind : kind + C]
    pix_halo.start()

    spread = spread_matrix()
    for r in range(4):
        cells = pix[r + 1, 1:17].reshape(256, C).astype(F32)
        taps = [earlier_frames(cells, 2).astype(BF), earlier_frames(cells, 1).astype(BF), cells.astype(BF)]
        shifted[r * 256 : (r + 1) * 256] = move_lanes(jnp.concatenate(taps, axis=1), spread)
    cot_halo.finish()
    for r in range(4):
        for b in range(3):
            for k in range(3):
                at = (b * 3 + k) * C
                xc[r * 256 : (r + 1) * 256, at : at + C] = cot[r + 2 - b, 2 - k : 18 - k].reshape(256, C)
    quarter = (iota((512, C), 0) >> 2) & 3
    extra = [tn(shifted[...], xc[:, k * C : (k + 1) * C]) for k in (7, 8)]
    for tile in range(7):
        total = tn(shifted[...], xc[:, tile * C : (tile + 1) * C])
        if tile < 6:
            total = jnp.where(quarter == 3, pltpu.roll(extra[tile // 3], 12 - 4 * (tile % 3), 0), total)
        conv.grads[:, :, :, :, tile * C : (tile + 1) * C] = total.astype(BF).reshape(4, 4, 2, 16, C)
    conv.grads[:, :, :, :, 7 * C :] = jnp.zeros((4, 4, 2, 16, C), BF)
    conv.start_core()
    for r in range(4):
        terms = nt(xc[r * 256 : (r + 1) * 256], wb[...])
        grad = terms[:, 2 * C :] + later_frames(terms[:, C : 2 * C], 1) + later_frames(terms[:, :C], 2)
        i, a = r // 2, r % 2
        for j in range(8):
            at = (i * 8 + j) * 16
            pre_pair = pre[at : at + 16, 2 * a * C : (2 * a + 2) * C]
            gate = 1.0 / (1.0 + jnp.exp(-pre_pair))
            slope = gate * (1.0 + pre_pair * (1.0 - gate))
            pair = jnp.concatenate([grad[2 * j * 16 : 2 * j * 16 + 16], grad[2 * j * 16 + 16 : 2 * j * 16 + 32]], axis=1)
            grad_pre[at : at + 16, 2 * a * C : (2 * a + 2) * C] = (pair * slope).astype(BF)
    conv.start_first()

    grad_merged[...] = nt(grad_pre[...], wup[...])
    low = grad_merged[...].astype(BF)
    grad_mixed = nt(low, wout[...]).astype(BF)
    grad_joined[:, 2 * E :] = tn(probs[...].astype(BF), grad_mixed).astype(BF)
    rest.grads[:, :, :, :, :E] = tn(merged[...], grad_pre[...]).astype(BF).reshape(4, 4, 2, 16, E)
    rest.grads[:, :, :, :, E : 2 * E] = tn(mixed[...], low).astype(BF).reshape(4, 4, 2, 16, E)
    rest.grads[:, :, :, :, 2 * E :] = tn(normed[...], grad_joined[:, 2 * E :]).astype(BF).reshape(4, 4, 2, 16, E)
    rest.start_core()

    grad_probs = nt(grad_mixed, values[...])
    inner = jnp.sum(probs[...] * grad_probs, axis=-1, keepdims=True)
    grad_scores = (probs[...] * (grad_probs - inner) * ROOT).astype(BF)
    grad_joined[:, :E] = norm_back(q_raw[...], nn(grad_scores, keys[...])).astype(BF)
    grad_joined[:, E : 2 * E] = norm_back(k_raw[...], tn(grad_scores, query[...])).astype(BF)
    rest.start_first()
    for part in range(2):
        at = part * E
        block = tn(normed[...], grad_joined[:, at : at + E])
        qk.grads[:, :, :, :, at : at + E] = block.astype(BF).reshape(4, 4, 2, 16, E)
    qk.start_core()

    grad_normed = nt(grad_joined[...], wqkv[...])
    states = norm_back(hs_send[...].reshape(256, E).astype(F32), grad_normed * gain_in[...])
    states = (grad_merged[...] + states).astype(BF)
    gs_send[...] = move(swap, states).reshape(8, 2, 16, E)
    qk.start_first()
    gs_copies = exchange(2, lambda to: gs_send.at[to], gs_recv)
    gs_recv[t] = gs_send[t]
    conv.start_second()

    pix_halo.finish()
    for r in range(4):
        taps = [pix[r + b, k : k + 16].reshape(256, C) for b in range(3) for k in range(3)]
        terms = nn(jnp.concatenate(taps, axis=1), wf[...])
        cells = terms[:, 2 * C :] + earlier_frames(terms[:, C : 2 * C], 1) + earlier_frames(terms[:, :C], 2)
        dec_send[:, :, r] = move(swap, cells.astype(BF)).reshape(8, 2, 16, C)
    dec_copies = exchange(3, lambda to: dec_send.at[to], dec_recv)
    dec_recv[t] = dec_send[t]

    rest.start_second()
    conv.start_rows()
    qk.start_second()
    rest.start_rows()
    qk.start_rows()
    conv.start_gather()
    rest.start_gather()
    qk.start_gather()
    for copy in gs_copies:
        copy.wait()
    states_out[...] = gs_recv[...]
    for copy in dec_copies:
        copy.wait()
    dec_out[...] = dec_recv[...]
    conv.wait()
    rest.wait()
    conv_out[...] = conv.total[...]
    rest_out[...] = rest.total[...]
    qk.wait()
    qk_out[...] = qk.total[...]


GROUPS = ((1024, 2), (1536, 2), (1024, 3))
SHARES = (
    jax.ShapeDtypeStruct((16, 1536), F32),
    jax.ShapeDtypeStruct((16, 512), F32),
    jax.ShapeDtypeStruct((16, 512), F32),
    jax.ShapeDtypeStruct((27, 4, 128), F32),
)


def finish_kernel(dec, states, conv_sum, rest_sum, qk_sum, decoded_out, states_out, qkv_out, out_out, up_out, conv_out):
    token_scale = 1.0 / 65536.0**0.5
    voxel_scale = 1.0 / 262144.0**0.5
    from_blocks = from_blocks_matrix()
    for f in range(2):
        states_out[f] = move(from_blocks, states[:, f].reshape(128, E)).reshape(2, 64, E)
    for k in range(8):
        decoded_out[:, :, k * 16 : (k + 1) * 16, :] = dec[k]

    def tile_of(total, tile):
        count = total.shape[2] // 128
        at = (tile % count) * 128
        return total[tile // count][:, at : at + 128].astype(F32)

    for tile in range(8):
        qkv_out[:, tile * 128 : (tile + 1) * 128] = tile_of(qk_sum, tile) * token_scale
    for tile in range(4):
        up_out[:, tile * 128 : (tile + 1) * 128] = tile_of(rest_sum, tile) * token_scale
        out_out[:, tile * 128 : (tile + 1) * 128] = tile_of(rest_sum, 4 + tile) * token_scale
        qkv_out[:, 2 * E + tile * 128 : 2 * E + (tile + 1) * 128] = tile_of(rest_sum, 8 + tile) * token_scale
    for tile in range(7):
        block = tile_of(conv_sum, tile) * voxel_scale
        for kind in range(4):
            piece = block[kind * 4 : kind * 4 + 4]
            if kind < 3:
                conv_out[kind * 9 + tile] = piece
            elif tile < 6:
                conv_out[(tile % 3) * 9 + 7 + tile // 3] = piece


def body(hidden_states, attn_gain, qkv_weight, out_weight, up_weight, conv_weight, cotangent):
    vmem = pl.BlockSpec(memory_space=pltpu.VMEM)
    hbm = pl.BlockSpec(memory_space=pl.ANY)
    scratch = [
        pltpu.VMEM((2, 2, 64, E), BF),
        pltpu.VMEM((8, 2, 16, E), BF),
        pltpu.VMEM((8, 2, 16, E), BF),
        pltpu.VMEM((8, 2, 4, 16, C), BF),
        pltpu.VMEM((E, 3 * E), BF),
        pltpu.VMEM((E, E), BF),
        pltpu.VMEM((E, E), BF),
        pltpu.VMEM((27, C, C), BF),
        pltpu.VMEM((9 * C, 3 * C), BF),
        pltpu.VMEM((3 * C, 9 * C), BF),
        pltpu.VMEM((6, 18, 16, C), BF),
        pltpu.VMEM((6, 18, 16, C), BF),
        pltpu.VMEM((1024, 9 * C), BF),
        pltpu.VMEM((1024, E), BF),
        pltpu.VMEM((256, E), BF),
        pltpu.VMEM((256, E), F32),
        pltpu.VMEM((256, E), F32),
        pltpu.VMEM((256, E), BF),
        pltpu.VMEM((256, E), BF),
        pltpu.VMEM((256, E), BF),
        pltpu.VMEM((256, 256), F32),
        pltpu.VMEM((256, E), BF),
        pltpu.VMEM((256, E), BF),
        pltpu.VMEM((256, E), F32),
        pltpu.VMEM((256, E), BF),
        pltpu.VMEM((256, E), F32),
        pltpu.VMEM((256, 3 * E), BF),
        pltpu.VMEM((8, 2, 4, 16, C), BF),
        pltpu.VMEM((8, 2, 4, 16, C), BF),
        pltpu.VMEM((8, 2, 16, E), BF),
        pltpu.VMEM((8, 2, 16, E), BF),
        pltpu.SemaphoreType.DMA((6,)),
        pltpu.SemaphoreType.DMA((4, 7)),
        pltpu.SemaphoreType.DMA((4, 7)),
        pltpu.SemaphoreType.DMA((2, 8)),
        pltpu.SemaphoreType.DMA((2, 8)),
    ]
    arrived = (
        jax.ShapeDtypeStruct((8, 2, 4, 16, C), BF),
        jax.ShapeDtypeStruct((8, 2, 16, E), BF),
    ) + tuple(jax.ShapeDtypeStruct((4, 16, width // 4), BF) for width, _ in GROUPS)
    results = pl.pallas_call(
        block_kernel,
        out_shape=arrived,
        in_specs=[hbm, vmem, hbm, hbm, hbm, hbm, hbm],
        out_specs=[vmem] * 5,
        scratch_shapes=scratch + [buffer for group in GROUPS for buffer in reducer_scratch(*group)],
        compiler_params=pltpu.CompilerParams(
            collective_id=0, has_side_effects=True, vmem_limit_bytes=56 * 2**20
        ),
    )(
        hidden_states,
        attn_gain.reshape(1, E),
        qkv_weight,
        out_weight,
        up_weight,
        conv_weight.reshape(27, C, C),
        cotangent,
    )
    decoded, states, qkv, out, up, conv = pl.pallas_call(
        finish_kernel,
        out_shape=(
            jax.ShapeDtypeStruct(cotangent.shape, BF),
            jax.ShapeDtypeStruct(hidden_states.shape, BF),
        )
        + SHARES,
        in_specs=[vmem] * 5,
        out_specs=[vmem] * 6,
    )(*results)
    return (decoded, states, qkv, out, up, conv.reshape(3, 3, 3, 4, C))


def solution(mesh):
    placed = (P("tm", "height", None, None), P(), P(), P(), P(), P(), P("tm", "height", None, None))
    return jax.shard_map(
        body,
        mesh=mesh,
        in_specs=placed,
        out_specs=(
            P("tm", "height", None, None),
            P("tm", "height", None, None),
            P("height", None),
            P("height", None),
            P("height", None),
            P(None, None, None, "height", None),
        ),
        check_vma=False,
    )
```

```python
import jax
import jax.numpy as jnp
from jax import lax
from jax.experimental import pallas as pl
from jax.experimental.pallas import tpu as pltpu
from jax.sharding import PartitionSpec as P

E = 512
C = 128
EPS = 1e-06
ROOT = 1.0 / 512.0**0.5

MESH = pl.DeviceIdType.MESH
BF = jnp.bfloat16
F32 = jnp.float32


def place():
    t = lax.axis_index("tm")
    h = lax.axis_index("height")
    return t, h, lax.rem(h, 2), lax.rem(h // 2, 4), h // 8


def block_of(t):
    return t + t // 4 * (11 - 2 * t)


def signal_peers(t, h):
    barrier = pltpu.get_barrier_semaphore()
    c, x, z = lax.rem(h, 2), lax.rem(h // 2, 4), h // 8
    y, far = lax.rem(t, 4), t // 4
    peers = [(lax.rem(t + k, 8), h) for k in range(1, 8)]
    peers += [(t, h + 1 - 2 * c)]
    peers += [(t, z * 8 + lax.rem(x + k, 4) * 2 + c) for k in range(1, 4)]
    for k in range(1, 8):
        to = lax.rem(far * 4 + z + k, 8)
        peers += [(to // 4 * 4 + y, lax.rem(to, 4) * 8 + x * 2 + c)]
    mine = block_of(t)
    peers += [(block_of(lax.rem(mine + i, 8)), lax.rem(h + j, 32)) for i in (7, 0, 1) for j in (31, 1)]
    for peer in peers:
        pl.semaphore_signal(barrier, inc=1, device_id=peer, device_id_type=MESH)
    return len(peers)


def remote(src, dst, send, recv, peer):
    return pltpu.make_async_remote_copy(
        src_ref=src, dst_ref=dst, send_sem=send, recv_sem=recv, device_id=peer, device_id_type=MESH
    )


class Reducer:
    def __init__(self, refs, where):
        self.grads, self.r1, self.r2x, self.r2y, self.s2x, self.s2y, self.r3x, self.r3y = refs[:8]
        self.s3, self.r4, self.total, self.send, self.recv = refs[8:]
        self.t, self.h, self.c, self.x, self.z = where
        self.y, self.far = lax.rem(self.t, 4), self.t // 4
        self.wide = self.grads.shape[-1] // 4
        self.by_x = self.s2x.shape[1]
        self.copies = []

    def start(self, index, src, dst, peer):
        copy = remote(src, dst, self.send.at[index], self.recv.at[index], peer)
        copy.start()
        self.copies.append(copy)

    def wait(self):
        for copy in self.copies:
            copy.wait()
        self.copies = []

    def x_peer(self, to):
        return (self.t, self.z * 8 + to * 2 + self.c)

    def y_peer(self, to):
        return (self.far * 4 + to, self.h)

    def start_core(self):
        c = self.c
        self.start(0, self.grads.at[:, :, 1 - c], self.r1, (self.t, self.h + 1 - 2 * c))

    def start_first(self):
        self.wait()
        c, wide = self.c, self.wide

        def add(i, carry):
            a, b = i // 4, lax.rem(i, 4)
            both = self.grads[a, b, c].astype(F32) + self.r1[a, b].astype(F32)
            self.grads[a, b, c] = both.astype(BF)
            return carry

        lax.fori_loop(0, 16, add, 0)
        for k in (2, 1, 3):
            to = lax.rem(self.x + k, 4)
            self.start(k, self.grads.at[pl.ds(0, self.by_x), to, c], self.r2x.at[k - 1], self.x_peer(to))
            to = lax.rem(self.y + k, 4)
            columns = pl.ds(pl.multiple_of(to * wide, 128), wide)
            self.start(3 + k, self.grads.at[pl.ds(self.by_x, 4 - self.by_x), :, c, :, columns], self.r2y.at[k - 1], self.y_peer(to))

    def start_second(self):
        self.wait()
        c, wide = self.c, self.wide
        for i in range(self.by_x):
            both = self.grads[i, self.x, c].astype(F32)
            for k in range(3):
                both = both + self.r2x[k, i].astype(F32)
            both = both.astype(BF)
            for q in range(4):
                self.s2x[q, i] = both[:, q * wide : (q + 1) * wide]
        columns = pl.ds(pl.multiple_of(self.y * wide, 128), wide)
        for i in range(4 - self.by_x):
            for q in range(4):
                both = self.grads[self.by_x + i, q, c, :, columns].astype(F32)
                for k in range(3):
                    both = both + self.r2y[k, i, q].astype(F32)
                self.s2y[q, i] = both.astype(BF)
        for k in (2, 1, 3):
            to = lax.rem(self.y + k, 4)
            self.start(6 + k, self.s2x.at[to], self.r3x.at[k - 1], self.y_peer(to))
            to = lax.rem(self.x + k, 4)
            self.start(9 + k, self.s2y.at[to], self.r3y.at[k - 1], self.x_peer(to))

    def start_rows(self):
        self.wait()
        for i in range(4):
            parts, at = (self.r3x, i) if i < self.by_x else (self.r3y, i - self.by_x)
            both = (self.s2x[self.y, at] if i < self.by_x else self.s2y[self.x, at]).astype(F32)
            for k in range(3):
                both = both + parts[k, at].astype(F32)
            self.s3[i] = both.astype(BF)
        for k in (4, 3, 5, 2, 6, 1, 7):
            to = lax.rem(self.far * 4 + self.z + k, 8)
            far, z = to // 4, lax.rem(to, 4)
            peer = (far * 4 + self.y, z * 8 + self.x * 2 + self.c)
            self.start(12 + k, self.s3.at[z], self.r4.at[k - 1], peer)

    def start_gather(self):
        self.wait()
        both = self.s3[self.z].astype(F32)
        for k in range(7):
            both = both + self.r4[k].astype(F32)
        self.total[self.y] = both.astype(BF)
        for k in (2, 1, 3):
            to = lax.rem(self.y + k, 4)
            self.start(19 + k, self.total.at[self.y], self.total.at[self.y], self.y_peer(to))


def reducer_scratch(width, by_x):
    wide, by_y = width // 4, 4 - by_x
    return [
        pltpu.VMEM((4, 4, 2, 16, width), BF),
        pltpu.VMEM((4, 4, 16, width), BF),
        pltpu.VMEM((3, by_x, 16, width), BF),
        pltpu.VMEM((3, by_y, 4, 16, wide), BF),
        pltpu.VMEM((4, by_x, 16, wide), BF),
        pltpu.VMEM((4, by_y, 16, wide), BF),
        pltpu.VMEM((3, by_x, 16, wide), BF),
        pltpu.VMEM((3, by_y, 16, wide), BF),
        pltpu.VMEM((4, 16, wide), BF),
        pltpu.VMEM((7, 16, wide), BF),
        pltpu.VMEM((4, 16, wide), BF),
        pltpu.SemaphoreType.DMA((23,)),
        pltpu.SemaphoreType.DMA((23,)),
    ]


def nn(a, b):
    return jnp.dot(a, b, preferred_element_type=F32)


def nt(a, b):
    return lax.dot_general(a, b, (((1,), (1,)), ((), ())), preferred_element_type=F32)


def tn(a, b):
    return lax.dot_general(a, b, (((0,), (0,)), ((), ())), preferred_element_type=F32)


def iota(shape, dim):
    return lax.broadcasted_iota(jnp.int32, shape, dim)


def ones_where(cond):
    return jnp.where(cond, 1.0, 0.0).astype(BF)


def swap_matrix():
    r, s = iota((256, 256), 0), iota((256, 256), 1)
    return ones_where(s == (r & 15) * 16 + (r >> 4))


def to_blocks_matrix():
    r, s = iota((128, 128), 0), iota((128, 128), 1)
    return ones_where(s == ((r >> 3) & 1) * 64 + (r >> 4) * 8 + (r & 7))


def from_blocks_matrix():
    r, s = iota((128, 128), 0), iota((128, 128), 1)
    return ones_where(s == ((r >> 3) & 7) * 16 + (r >> 6) * 8 + (r & 7))


def spread_matrix():
    r, s = iota((512, 384), 1), iota((512, 384), 0)
    channel = r & 127
    return ones_where(s == (channel >> 2) * 16 + (r >> 7) * 4 + (channel & 3))


def move(matrix, rows):
    return nn(matrix, rows).astype(BF)


def rms_scale(rows):
    return lax.rsqrt(jnp.mean(rows * rows, axis=-1, keepdims=True) + EPS)


def norm_back(rows, upstream):
    factor = rms_scale(rows)
    unit = rows * factor
    return factor * (upstream - unit * jnp.mean(upstream * unit, axis=-1, keepdims=True))


def later_frames(rows, by):
    count = rows.shape[0]
    frame = iota(rows.shape, 0) & 15
    return jnp.where(frame + by <= 15, pltpu.roll(rows, count - by, 0), 0.0)


def earlier_frames(rows, by):
    frame = iota(rows.shape, 0) & 15
    return jnp.where(frame >= by, pltpu.roll(rows, by, 0), 0.0)


class Halo:
    def __init__(self, cells, send, recv, t, h):
        mine = block_of(t)
        self.cells, self.block, self.h = cells, mine, h
        inner = {-1: (pl.ds(1, 1), pl.ds(1, 1)), 0: (pl.ds(1, 4), pl.ds(1, 16)), 1: (pl.ds(4, 1), pl.ds(16, 1))}
        outer = {-1: (pl.ds(5, 1), pl.ds(17, 1)), 0: (pl.ds(1, 4), pl.ds(1, 16)), 1: (pl.ds(0, 1), pl.ds(0, 1))}
        self.copies = []
        for i in (-1, 0, 1):
            for j in (-1, 0, 1):
                if i or j:
                    at = len(self.copies)
                    peer = (block_of(lax.rem(mine + 8 + j, 8)), lax.rem(h + 32 + i, 32))
                    src = cells.at[inner[i][0], inner[j][1]]
                    dst = cells.at[outer[i][0], outer[j][1]]
                    self.copies.append(remote(src, dst, send.at[at], recv.at[at], peer))

    def start(self):
        for copy in self.copies:
            copy.start()

    def finish(self):
        for copy in self.copies:
            copy.wait()
        side, edge = jnp.zeros((6, 16, C), BF), jnp.zeros((18, 16, C), BF)

        @pl.when(self.block == 0)
        def _():
            self.cells[:, 0] = side

        @pl.when(self.block == 7)
        def _():
            self.cells[:, 17] = side

        @pl.when(self.h == 0)
        def _():
            self.cells[0] = edge

        @pl.when(self.h == 31)
        def _():
            self.cells[5] = edge


def block_kernel(
    hs_hbm, gain_in, wqkv_in, wout_in, wup_in, wconv_in, cot_in,
    dec_out, states_out, conv_out, rest_out, qk_out,
    hs_in, hs_send, hs_recv, cot_recv, wqkv, wout, wup, wconv, wf, wb,
    cot, pix, xc, shifted, normed, q_raw, k_raw, query, keys, values, probs, mixed, merged, pre,
    grad_pre, grad_merged, grad_joined, dec_send, dec_recv, gs_send, gs_recv,
    load_sem, a2a_send, a2a_recv, halo_send, halo_recv,
    *reducers,
):
    t, h, c, x, z = place()
    mine = block_of(t)
    expected = signal_peers(t, h)
    conv, rest, qk = (Reducer(reducers[13 * i : 13 * i + 13], (t, h, c, x, z)) for i in range(3))
    loads = [
        pltpu.make_async_copy(src, dst, load_sem.at[i])
        for i, (src, dst) in enumerate(
            (
                (hs_hbm, hs_in),
                (cot_in.at[:, :, pl.ds(pl.multiple_of(mine * 16, 16), 16), :], cot_recv.at[t]),
                (wconv_in, wconv),
                (wqkv_in, wqkv),
                (wout_in, wout),
                (wup_in, wup),
            )
        )
    ]
    for load in loads:
        load.start()
    pl.semaphore_wait(pltpu.get_barrier_semaphore(), expected)

    def exchange(kind, src_of, dst, slot):
        copies = []
        for k in (4, 3, 5, 2, 6, 1, 7):
            to = lax.rem(t + k, 8)
            copy = remote(src_of(to), dst.at[slot], a2a_send.at[kind, k - 1], a2a_recv.at[kind, k - 1], (to, h))
            copy.start()
            copies.append(copy)
        return copies

    cot_copies = exchange(
        1, lambda to: cot_in.at[:, :, pl.ds(pl.multiple_of(block_of(to) * 16, 16), 16), :], cot_recv, t
    )
    swap = swap_matrix()
    to_blocks = to_blocks_matrix()
    loads[0].wait()
    for f in range(2):
        moved = move(to_blocks, hs_in[f].reshape(128, E))
        hs_send[:, f] = moved.reshape(8, 16, E)

    hs_copies = exchange(0, lambda to: hs_send.at[block_of(to)], hs_recv, t)
    hs_recv[t] = hs_send[mine]
    cot_halo = Halo(cot, halo_send.at[0], halo_recv.at[0], t, h)
    pix_halo = Halo(pix, halo_send.at[1], halo_recv.at[1], t, h)

    loads[1].wait()
    loads[2].wait()
    for a in range(3):
        for k in range(9):
            tap = wconv[a * 9 + k]
            wf[k * C : (k + 1) * C, a * C : (a + 1) * C] = tap
            wb[a * C : (a + 1) * C, k * C : (k + 1) * C] = tap
    for load in loads[3:]:
        load.wait()

    for copy in cot_copies:
        copy.wait()
    for r in range(4):
        cells = move(swap, cot_recv[:, :, r].reshape(256, C))
        cot[r + 1, 1:17] = cells.reshape(16, 16, C)
    cot_halo.start()

    for copy in hs_copies:
        copy.wait()
    tokens = move(swap, hs_recv[...].reshape(256, E))
    hs_send[...] = tokens.reshape(8, 2, 16, E)
    wide = tokens.astype(F32)
    normed[...] = (wide * rms_scale(wide) * gain_in[...]).astype(BF)
    q_raw[...] = nn(normed[...], wqkv[:, :E])
    k_raw[...] = nn(normed[...], wqkv[:, E : 2 * E])
    values[...] = nn(normed[...], wqkv[:, 2 * E :]).astype(BF)
    raw = q_raw[...]
    query[...] = (raw * rms_scale(raw)).astype(BF)
    raw = k_raw[...]
    keys[...] = (raw * rms_scale(raw)).astype(BF)

    rows, cols = iota((256, 256), 0), iota((256, 256), 1)
    allowed = ((rows >> 4) == (cols >> 4)) & (cols <= rows)
    weights = jnp.where(allowed, jnp.exp(nt(query[...], keys[...]) * ROOT), 0.0)
    probs[...] = weights / jnp.sum(weights, axis=-1, keepdims=True)
    mixed[...] = nn(probs[...].astype(BF), values[...]).astype(BF)

    tokens_wide = hs_send[...].reshape(256, E).astype(F32)
    merged[...] = (tokens_wide + nn(mixed[...], wout[...])).astype(BF)
    pre[...] = nn(merged[...], wup[...])
    act = pre[...]
    act = (act / (1.0 + jnp.exp(-act))).astype(BF)
    for i in range(2):
        for a in range(2):
            for j in range(8):
                for b in range(2):
                    at = (i * 8 + j) * 16
                    kind = (2 * a + b) * C
                    pix[2 * i + a + 1, 2 * j + b + 1] = act[at : at + 16, kind : kind + C]
    pix_halo.start()

    spread = spread_matrix()
    for r in range(4):
        cells = pix[r + 1, 1:17].reshape(256, C).astype(F32)
        taps = [earlier_frames(cells, 2).astype(BF), earlier_frames(cells, 1).astype(BF), cells.astype(BF)]
        shifted[:, r * 256 : (r + 1) * 256] = nt(spread, jnp.concatenate(taps, axis=1)).astype(BF)
    cot_halo.finish()
    for r in range(4):
        for b in range(3):
            for k in range(3):
                at = (b * 3 + k) * C
                xc[r * 256 : (r + 1) * 256, at : at + C] = cot[r + 2 - b, 2 - k : 18 - k].reshape(256, C)
    quarter = (iota((512, C), 0) >> 2) & 3
    extra = nn(shifted[...], xc[:, 7 * C :])
    for pair in range(4):
        tiles = (2 * pair, 2 * pair + 1) if pair < 3 else (6,)
        totals = nn(shifted[...], xc[:, 2 * pair * C : min(2 * pair + 2, 7) * C])
        for at, tile in enumerate(tiles):
            total = totals[:, at * C : (at + 1) * C]
            if tile < 6:
                late = extra[:, (tile // 3) * C : (tile // 3 + 1) * C]
                total = jnp.where(quarter == 3, pltpu.roll(late, 12 - 4 * (tile % 3), 0), total)
            conv.grads[:, :, :, :, tile * C : (tile + 1) * C] = total.astype(BF).reshape(4, 4, 2, 16, C)
    conv.grads[:, :, :, :, 7 * C :] = jnp.zeros((4, 4, 2, 16, C), BF)
    conv.start_core()
    for r in range(4):
        terms = nt(xc[r * 256 : (r + 1) * 256], wb[...])
        grad = terms[:, 2 * C :] + later_frames(terms[:, C : 2 * C], 1) + later_frames(terms[:, :C], 2)
        i, a = r // 2, r % 2
        for j in range(8):
            at = (i * 8 + j) * 16
            pre_pair = pre[at : at + 16, 2 * a * C : (2 * a + 2) * C]
            gate = 1.0 / (1.0 + jnp.exp(-pre_pair))
            slope = gate * (1.0 + pre_pair * (1.0 - gate))
            pair = jnp.concatenate([grad[2 * j * 16 : 2 * j * 16 + 16], grad[2 * j * 16 + 16 : 2 * j * 16 + 32]], axis=1)
            grad_pre[at : at + 16, 2 * a * C : (2 * a + 2) * C] = (pair * slope).astype(BF)
    conv.start_first()

    grad_merged[...] = nt(grad_pre[...], wup[...])
    low = grad_merged[...].astype(BF)
    grad_mixed = nt(low, wout[...]).astype(BF)
    grad_joined[:, 2 * E :] = tn(probs[...].astype(BF), grad_mixed).astype(BF)
    rest.grads[:, :, :, :, :E] = tn(merged[...], grad_pre[...]).astype(BF).reshape(4, 4, 2, 16, E)
    rest.grads[:, :, :, :, E : 2 * E] = tn(mixed[...], low).astype(BF).reshape(4, 4, 2, 16, E)
    rest.grads[:, :, :, :, 2 * E :] = tn(normed[...], grad_joined[:, 2 * E :]).astype(BF).reshape(4, 4, 2, 16, E)
    rest.start_core()

    grad_probs = nt(grad_mixed, values[...])
    inner = jnp.sum(probs[...] * grad_probs, axis=-1, keepdims=True)
    grad_scores = (probs[...] * (grad_probs - inner) * ROOT).astype(BF)
    grad_joined[:, :E] = norm_back(q_raw[...], nn(grad_scores, keys[...])).astype(BF)
    grad_joined[:, E : 2 * E] = norm_back(k_raw[...], tn(grad_scores, query[...])).astype(BF)
    rest.start_first()
    qk.grads[...] = tn(normed[...], grad_joined[:, : 2 * E]).astype(BF).reshape(4, 4, 2, 16, 2 * E)
    qk.start_core()

    grad_normed = nt(grad_joined[...], wqkv[...])
    states = norm_back(hs_send[...].reshape(256, E).astype(F32), grad_normed * gain_in[...])
    states = (grad_merged[...] + states).astype(BF)
    gs_send[...] = move(swap, states).reshape(8, 2, 16, E)
    qk.start_first()
    gs_copies = exchange(2, lambda to: gs_send.at[to], gs_recv, mine)
    gs_recv[mine] = gs_send[t]
    pix_halo.finish()
    for r in range(4):
        taps = [pix[r + b, k : k + 16].reshape(256, C) for b in range(3) for k in range(3)]
        terms = nn(jnp.concatenate(taps, axis=1), wf[...])
        cells = terms[:, 2 * C :] + earlier_frames(terms[:, C : 2 * C], 1) + earlier_frames(terms[:, :C], 2)
        dec_send[:, :, r] = move(swap, cells.astype(BF)).reshape(8, 2, 16, C)
    dec_copies = exchange(3, lambda to: dec_send.at[to], dec_recv, mine)
    dec_recv[mine] = dec_send[t]
    conv.start_second()
    qk.start_second()
    rest.start_second()
    conv.start_rows()
    qk.start_rows()
    rest.start_rows()
    conv.start_gather()
    qk.start_gather()
    rest.start_gather()
    for copy in gs_copies:
        copy.wait()
    states_out[...] = gs_recv[...]
    for copy in dec_copies:
        copy.wait()
    dec_out[...] = dec_recv[...]
    conv.wait()
    rest.wait()
    conv_out[...] = conv.total[...]
    rest_out[...] = rest.total[...]
    qk.wait()
    qk_out[...] = qk.total[...]


GROUPS = ((1024, 2), (1536, 2), (1024, 3))
SHARES = (
    jax.ShapeDtypeStruct((16, 1536), F32),
    jax.ShapeDtypeStruct((16, 512), F32),
    jax.ShapeDtypeStruct((16, 512), F32),
    jax.ShapeDtypeStruct((27, 4, 128), F32),
)


def finish_kernel(dec, states, conv_sum, rest_sum, qk_sum, decoded_out, states_out, qkv_out, out_out, up_out, conv_out):
    token_scale = 1.0 / 65536.0**0.5
    voxel_scale = 1.0 / 262144.0**0.5
    from_blocks = from_blocks_matrix()
    for f in range(2):
        states_out[f] = move(from_blocks, states[:, f].reshape(128, E)).reshape(2, 64, E)
    for k in range(8):
        decoded_out[:, :, k * 16 : (k + 1) * 16, :] = dec[k]

    def tile_of(total, tile):
        count = total.shape[2] // 128
        at = (tile % count) * 128
        return total[tile // count][:, at : at + 128].astype(F32)

    for tile in range(8):
        qkv_out[:, tile * 128 : (tile + 1) * 128] = tile_of(qk_sum, tile) * token_scale
    for tile in range(4):
        up_out[:, tile * 128 : (tile + 1) * 128] = tile_of(rest_sum, tile) * token_scale
        out_out[:, tile * 128 : (tile + 1) * 128] = tile_of(rest_sum, 4 + tile) * token_scale
        qkv_out[:, 2 * E + tile * 128 : 2 * E + (tile + 1) * 128] = tile_of(rest_sum, 8 + tile) * token_scale
    for tile in range(7):
        block = tile_of(conv_sum, tile) * voxel_scale
        for kind in range(4):
            piece = block[kind * 4 : kind * 4 + 4]
            if kind < 3:
                conv_out[kind * 9 + tile] = piece
            elif tile < 6:
                conv_out[(tile % 3) * 9 + 7 + tile // 3] = piece


def body(hidden_states, attn_gain, qkv_weight, out_weight, up_weight, conv_weight, cotangent):
    vmem = pl.BlockSpec(memory_space=pltpu.VMEM)
    hbm = pl.BlockSpec(memory_space=pl.ANY)
    scratch = [
        pltpu.VMEM((2, 2, 64, E), BF),
        pltpu.VMEM((8, 2, 16, E), BF),
        pltpu.VMEM((8, 2, 16, E), BF),
        pltpu.VMEM((8, 2, 4, 16, C), BF),
        pltpu.VMEM((E, 3 * E), BF),
        pltpu.VMEM((E, E), BF),
        pltpu.VMEM((E, E), BF),
        pltpu.VMEM((27, C, C), BF),
        pltpu.VMEM((9 * C, 3 * C), BF),
        pltpu.VMEM((3 * C, 9 * C), BF),
        pltpu.VMEM((6, 18, 16, C), BF),
        pltpu.VMEM((6, 18, 16, C), BF),
        pltpu.VMEM((1024, 9 * C), BF),
        pltpu.VMEM((E, 1024), BF),
        pltpu.VMEM((256, E), BF),
        pltpu.VMEM((256, E), F32),
        pltpu.VMEM((256, E), F32),
        pltpu.VMEM((256, E), BF),
        pltpu.VMEM((256, E), BF),
        pltpu.VMEM((256, E), BF),
        pltpu.VMEM((256, 256), F32),
        pltpu.VMEM((256, E), BF),
        pltpu.VMEM((256, E), BF),
        pltpu.VMEM((256, E), F32),
        pltpu.VMEM((256, E), BF),
        pltpu.VMEM((256, E), F32),
        pltpu.VMEM((256, 3 * E), BF),
        pltpu.VMEM((8, 2, 4, 16, C), BF),
        pltpu.VMEM((8, 2, 4, 16, C), BF),
        pltpu.VMEM((8, 2, 16, E), BF),
        pltpu.VMEM((8, 2, 16, E), BF),
        pltpu.SemaphoreType.DMA((6,)),
        pltpu.SemaphoreType.DMA((4, 7)),
        pltpu.SemaphoreType.DMA((4, 7)),
        pltpu.SemaphoreType.DMA((2, 8)),
        pltpu.SemaphoreType.DMA((2, 8)),
    ]
    arrived = (
        jax.ShapeDtypeStruct((8, 2, 4, 16, C), BF),
        jax.ShapeDtypeStruct((8, 2, 16, E), BF),
    ) + tuple(jax.ShapeDtypeStruct((4, 16, width // 4), BF) for width, _ in GROUPS)
    results = pl.pallas_call(
        block_kernel,
        out_shape=arrived,
        in_specs=[hbm, vmem, hbm, hbm, hbm, hbm, hbm],
        out_specs=[vmem] * 5,
        scratch_shapes=scratch + [buffer for group in GROUPS for buffer in reducer_scratch(*group)],
        compiler_params=pltpu.CompilerParams(
            collective_id=0, has_side_effects=True, vmem_limit_bytes=56 * 2**20
        ),
    )(
        hidden_states,
        attn_gain.reshape(1, E),
        qkv_weight,
        out_weight,
        up_weight,
        conv_weight.reshape(27, C, C),
        cotangent,
    )
    decoded, states, qkv, out, up, conv = pl.pallas_call(
        finish_kernel,
        out_shape=(
            jax.ShapeDtypeStruct(cotangent.shape, BF),
            jax.ShapeDtypeStruct(hidden_states.shape, BF),
        )
        + SHARES,
        in_specs=[vmem] * 5,
        out_specs=[vmem] * 6,
    )(*results)
    return (decoded, states, qkv, out, up, conv.reshape(3, 3, 3, 4, C))


def solution(mesh):
    placed = (P("tm", "height", None, None), P(), P(), P(), P(), P(), P("tm", "height", None, None))
    return jax.shard_map(
        body,
        mesh=mesh,
        in_specs=placed,
        out_specs=(
            P("tm", "height", None, None),
            P("tm", "height", None, None),
            P("height", None),
            P("height", None),
            P("height", None),
            P(None, None, None, "height", None),
        ),
        check_vma=False,
    )
```

```python
import jax
import jax.numpy as jnp
from jax import lax
from jax.experimental import pallas as pl
from jax.experimental.pallas import tpu as pltpu
from jax.sharding import PartitionSpec as P

E = 512
C = 128
EPS = 1e-06
ROOT = 1.0 / 512.0**0.5

MESH = pl.DeviceIdType.MESH
BF = jnp.bfloat16
F32 = jnp.float32


def place():
    t = lax.axis_index("tm")
    h = lax.axis_index("height")
    return t, h, lax.rem(h, 2), lax.rem(h // 2, 4), h // 8


def block_of(t):
    return t + t // 4 * (11 - 2 * t)


def signal_peers(t, h):
    barrier = pltpu.get_barrier_semaphore()
    c, x, z = lax.rem(h, 2), lax.rem(h // 2, 4), h // 8
    y, far = lax.rem(t, 4), t // 4
    peers = [(lax.rem(t + k, 8), h) for k in range(1, 8)]
    peers += [(t, h + 1 - 2 * c)]
    peers += [(t, z * 8 + lax.rem(x + k, 4) * 2 + c) for k in range(1, 4)]
    for k in range(1, 8):
        to = lax.rem(far * 4 + z + k, 8)
        peers += [(to // 4 * 4 + y, lax.rem(to, 4) * 8 + x * 2 + c)]
    mine = block_of(t)
    peers += [(block_of(lax.rem(mine + i, 8)), lax.rem(h + j, 32)) for i in (7, 0, 1) for j in (31, 1)]
    for peer in peers:
        pl.semaphore_signal(barrier, inc=1, device_id=peer, device_id_type=MESH)
    return len(peers)


def remote(src, dst, send, recv, peer):
    return pltpu.make_async_remote_copy(
        src_ref=src, dst_ref=dst, send_sem=send, recv_sem=recv, device_id=peer, device_id_type=MESH
    )


class Reducer:
    def __init__(self, refs, where):
        self.grads, self.r1, self.r2x, self.r2y, self.s2x, self.s2y, self.r3x, self.r3y = refs[:8]
        self.s3, self.r4, self.total, self.send, self.recv = refs[8:]
        self.t, self.h, self.c, self.x, self.z = where
        self.y, self.far = lax.rem(self.t, 4), self.t // 4
        self.wide = self.grads.shape[-1] // 4
        self.by_x = self.s2x.shape[1]
        self.copies = []

    def start(self, index, src, dst, peer):
        copy = remote(src, dst, self.send.at[index], self.recv.at[index], peer)
        copy.start()
        self.copies.append(copy)

    def wait(self):
        for copy in self.copies:
            copy.wait()
        self.copies = []

    def x_peer(self, to):
        return (self.t, self.z * 8 + to * 2 + self.c)

    def y_peer(self, to):
        return (self.far * 4 + to, self.h)

    def start_core(self):
        c = self.c
        self.start(0, self.grads.at[:, :, 1 - c], self.r1, (self.t, self.h + 1 - 2 * c))

    def start_first(self):
        self.wait()
        c, wide = self.c, self.wide

        def add(i, carry):
            a, b = i // 4, lax.rem(i, 4)
            both = self.grads[a, b, c].astype(F32) + self.r1[a, b].astype(F32)
            self.grads[a, b, c] = both.astype(BF)
            return carry

        lax.fori_loop(0, 16, add, 0)
        for k in (2, 1, 3):
            to = lax.rem(self.x + k, 4)
            self.start(k, self.grads.at[pl.ds(0, self.by_x), to, c], self.r2x.at[k - 1], self.x_peer(to))
            to = lax.rem(self.y + k, 4)
            columns = pl.ds(pl.multiple_of(to * wide, 128), wide)
            self.start(3 + k, self.grads.at[pl.ds(self.by_x, 4 - self.by_x), :, c, :, columns], self.r2y.at[k - 1], self.y_peer(to))

    def start_second(self):
        self.wait()
        c, wide = self.c, self.wide
        for i in range(self.by_x):
            both = self.grads[i, self.x, c].astype(F32)
            for k in range(3):
                both = both + self.r2x[k, i].astype(F32)
            both = both.astype(BF)
            for q in range(4):
                self.s2x[q, i] = both[:, q * wide : (q + 1) * wide]
        columns = pl.ds(pl.multiple_of(self.y * wide, 128), wide)
        for i in range(4 - self.by_x):
            for q in range(4):
                both = self.grads[self.by_x + i, q, c, :, columns].astype(F32)
                for k in range(3):
                    both = both + self.r2y[k, i, q].astype(F32)
                self.s2y[q, i] = both.astype(BF)
        for k in (2, 1, 3):
            to = lax.rem(self.y + k, 4)
            self.start(6 + k, self.s2x.at[to], self.r3x.at[k - 1], self.y_peer(to))
            to = lax.rem(self.x + k, 4)
            self.start(9 + k, self.s2y.at[to], self.r3y.at[k - 1], self.x_peer(to))

    def start_rows(self):
        self.wait()
        for i in range(4):
            parts, at = (self.r3x, i) if i < self.by_x else (self.r3y, i - self.by_x)
            both = (self.s2x[self.y, at] if i < self.by_x else self.s2y[self.x, at]).astype(F32)
            for k in range(3):
                both = both + parts[k, at].astype(F32)
            self.s3[i] = both.astype(BF)
        for k in (4, 3, 5, 2, 6, 1, 7):
            to = lax.rem(self.far * 4 + self.z + k, 8)
            far, z = to // 4, lax.rem(to, 4)
            peer = (far * 4 + self.y, z * 8 + self.x * 2 + self.c)
            self.start(12 + k, self.s3.at[z], self.r4.at[k - 1], peer)

    def start_gather(self):
        self.wait()
        both = self.s3[self.z].astype(F32)
        for k in range(7):
            both = both + self.r4[k].astype(F32)
        self.total[self.y] = both.astype(BF)
        for k in (2, 1, 3):
            to = lax.rem(self.y + k, 4)
            self.start(19 + k, self.total.at[self.y], self.total.at[self.y], self.y_peer(to))


def reducer_scratch(width, by_x):
    wide, by_y = width // 4, 4 - by_x
    return [
        pltpu.VMEM((4, 4, 2, 16, width), BF),
        pltpu.VMEM((4, 4, 16, width), BF),
        pltpu.VMEM((3, by_x, 16, width), BF),
        pltpu.VMEM((3, by_y, 4, 16, wide), BF),
        pltpu.VMEM((4, by_x, 16, wide), BF),
        pltpu.VMEM((4, by_y, 16, wide), BF),
        pltpu.VMEM((3, by_x, 16, wide), BF),
        pltpu.VMEM((3, by_y, 16, wide), BF),
        pltpu.VMEM((4, 16, wide), BF),
        pltpu.VMEM((7, 16, wide), BF),
        pltpu.VMEM((4, 16, wide), BF),
        pltpu.SemaphoreType.DMA((23,)),
        pltpu.SemaphoreType.DMA((23,)),
    ]


def nn(a, b):
    return jnp.dot(a, b, preferred_element_type=F32)


def nt(a, b):
    return lax.dot_general(a, b, (((1,), (1,)), ((), ())), preferred_element_type=F32)


def tn(a, b):
    return lax.dot_general(a, b, (((0,), (0,)), ((), ())), preferred_element_type=F32)


def iota(shape, dim):
    return lax.broadcasted_iota(jnp.int32, shape, dim)


def ones_where(cond):
    return jnp.where(cond, 1.0, 0.0).astype(BF)


def swap_matrix():
    r, s = iota((256, 256), 0), iota((256, 256), 1)
    return ones_where(s == (r & 15) * 16 + (r >> 4))


def to_blocks_matrix():
    r, s = iota((128, 128), 0), iota((128, 128), 1)
    return ones_where(s == ((r >> 3) & 1) * 64 + (r >> 4) * 8 + (r & 7))


def from_blocks_matrix():
    r, s = iota((128, 128), 0), iota((128, 128), 1)
    return ones_where(s == ((r >> 3) & 7) * 16 + (r >> 6) * 8 + (r & 7))


def spread_matrix():
    r, s = iota((512, 384), 1), iota((512, 384), 0)
    channel = r & 127
    return ones_where(s == (channel >> 2) * 16 + (r >> 7) * 4 + (channel & 3))


def move(matrix, rows):
    return nn(matrix, rows).astype(BF)


def rms_scale(rows):
    return lax.rsqrt(jnp.mean(rows * rows, axis=-1, keepdims=True) + EPS)


def norm_back(rows, upstream):
    factor = rms_scale(rows)
    unit = rows * factor
    return factor * (upstream - unit * jnp.mean(upstream * unit, axis=-1, keepdims=True))


def later_frames(rows, by):
    count = rows.shape[0]
    frame = iota(rows.shape, 0) & 15
    return jnp.where(frame + by <= 15, pltpu.roll(rows, count - by, 0), 0.0)


def earlier_frames(rows, by):
    frame = iota(rows.shape, 0) & 15
    return jnp.where(frame >= by, pltpu.roll(rows, by, 0), 0.0)


class Halo:
    def __init__(self, cells, send, recv, t, h):
        mine = block_of(t)
        self.cells, self.block, self.h = cells, mine, h
        inner = {-1: (pl.ds(1, 1), pl.ds(1, 1)), 0: (pl.ds(1, 4), pl.ds(1, 16)), 1: (pl.ds(4, 1), pl.ds(16, 1))}
        outer = {-1: (pl.ds(5, 1), pl.ds(17, 1)), 0: (pl.ds(1, 4), pl.ds(1, 16)), 1: (pl.ds(0, 1), pl.ds(0, 1))}
        self.copies = []
        for i in (-1, 0, 1):
            for j in (-1, 0, 1):
                if i or j:
                    at = len(self.copies)
                    peer = (block_of(lax.rem(mine + 8 + j, 8)), lax.rem(h + 32 + i, 32))
                    src = cells.at[inner[i][0], inner[j][1]]
                    dst = cells.at[outer[i][0], outer[j][1]]
                    self.copies.append(remote(src, dst, send.at[at], recv.at[at], peer))

    def start(self):
        for copy in self.copies:
            copy.start()

    def finish(self):
        for copy in self.copies:
            copy.wait()
        side, edge = jnp.zeros((6, 16, C), BF), jnp.zeros((18, 16, C), BF)

        @pl.when(self.block == 0)
        def _():
            self.cells[:, 0] = side

        @pl.when(self.block == 7)
        def _():
            self.cells[:, 17] = side

        @pl.when(self.h == 0)
        def _():
            self.cells[0] = edge

        @pl.when(self.h == 31)
        def _():
            self.cells[5] = edge


def block_kernel(
    hs_hbm, gain_in, wqkv_in, wout_in, wup_in, wconv_in, cot_in,
    dec_out, states_out, conv_out, rest_out, qk_out,
    hs_in, hs_send, hs_recv, cot_recv, wqkv, wout, wup, wconv, wf, wb,
    cot, pix, xc, shifted, normed, q_raw, k_raw, query, keys, values, probs, mixed, merged, pre,
    grad_pre, grad_merged, grad_joined, dec_send, dec_recv, gs_send, gs_recv,
    load_sem, a2a_send, a2a_recv, halo_send, halo_recv,
    *reducers,
):
    t, h, c, x, z = place()
    mine = block_of(t)
    expected = signal_peers(t, h)
    conv, rest, qk = (Reducer(reducers[13 * i : 13 * i + 13], (t, h, c, x, z)) for i in range(3))
    loads = [
        pltpu.make_async_copy(src, dst, load_sem.at[i])
        for i, (src, dst) in enumerate(
            (
                (hs_hbm, hs_in),
                (cot_in.at[:, :, pl.ds(pl.multiple_of(mine * 16, 16), 16), :], cot_recv.at[t]),
                (wconv_in, wconv),
                (wqkv_in, wqkv),
                (wout_in, wout),
                (wup_in, wup),
            )
        )
    ]
    for load in loads:
        load.start()
    pl.semaphore_wait(pltpu.get_barrier_semaphore(), expected)

    def exchange(kind, src_of, dst, slot):
        copies = []
        for k in (4, 3, 5, 2, 6, 1, 7):
            to = lax.rem(t + k, 8)
            copy = remote(src_of(to), dst.at[slot], a2a_send.at[kind, k - 1], a2a_recv.at[kind, k - 1], (to, h))
            copy.start()
            copies.append(copy)
        return copies

    cot_copies = exchange(
        1, lambda to: cot_in.at[:, :, pl.ds(pl.multiple_of(block_of(to) * 16, 16), 16), :], cot_recv, t
    )
    swap = swap_matrix()
    to_blocks = to_blocks_matrix()
    loads[0].wait()
    for f in range(2):
        moved = move(to_blocks, hs_in[f].reshape(128, E))
        hs_send[:, f] = moved.reshape(8, 16, E)

    hs_copies = exchange(0, lambda to: hs_send.at[block_of(to)], hs_recv, t)
    hs_recv[t] = hs_send[mine]
    cot_halo = Halo(cot, halo_send.at[0], halo_recv.at[0], t, h)
    pix_halo = Halo(pix, halo_send.at[1], halo_recv.at[1], t, h)

    loads[1].wait()
    loads[2].wait()
    for a in range(3):
        for k in range(9):
            tap = wconv[a * 9 + k]
            wf[k * C : (k + 1) * C, a * C : (a + 1) * C] = tap
            wb[a * C : (a + 1) * C, k * C : (k + 1) * C] = tap
    for load in loads[3:]:
        load.wait()

    for copy in cot_copies:
        copy.wait()
    for r in range(4):
        cells = move(swap, cot_recv[:, :, r].reshape(256, C))
        cot[r + 1, 1:17] = cells.reshape(16, 16, C)
    cot_halo.start()

    for copy in hs_copies:
        copy.wait()
    tokens = move(swap, hs_recv[...].reshape(256, E))
    hs_send[...] = tokens.reshape(8, 2, 16, E)
    wide = tokens.astype(F32)
    normed[...] = (wide * rms_scale(wide) * gain_in[...]).astype(BF)
    q_raw[...] = nn(normed[...], wqkv[:, :E])
    k_raw[...] = nn(normed[...], wqkv[:, E : 2 * E])
    values[...] = nn(normed[...], wqkv[:, 2 * E :]).astype(BF)
    raw = q_raw[...]
    query[...] = (raw * rms_scale(raw)).astype(BF)
    raw = k_raw[...]
    keys[...] = (raw * rms_scale(raw)).astype(BF)

    rows, cols = iota((256, 256), 0), iota((256, 256), 1)
    allowed = ((rows >> 4) == (cols >> 4)) & (cols <= rows)
    weights = jnp.where(allowed, jnp.exp(nt(query[...], keys[...]) * ROOT), 0.0)
    probs[...] = weights / jnp.sum(weights, axis=-1, keepdims=True)
    mixed[...] = nn(probs[...].astype(BF), values[...]).astype(BF)

    tokens_wide = hs_send[...].reshape(256, E).astype(F32)
    merged[...] = (tokens_wide + nn(mixed[...], wout[...])).astype(BF)
    pre[...] = nn(merged[...], wup[...])
    act = pre[...]
    act = (act / (1.0 + jnp.exp(-act))).astype(BF)
    for i in range(2):
        for a in range(2):
            for j in range(8):
                for b in range(2):
                    at = (i * 8 + j) * 16
                    kind = (2 * a + b) * C
                    pix[2 * i + a + 1, 2 * j + b + 1] = act[at : at + 16, kind : kind + C]
    pix_halo.start()

    spread = spread_matrix()
    for r in range(4):
        cells = pix[r + 1, 1:17].reshape(256, C).astype(F32)
        taps = [earlier_frames(cells, 2).astype(BF), earlier_frames(cells, 1).astype(BF), cells.astype(BF)]
        shifted[:, r * 256 : (r + 1) * 256] = nt(spread, jnp.concatenate(taps, axis=1)).astype(BF)
    cot_halo.finish()
    for r in range(4):
        for b in range(3):
            for k in range(3):
                at = (b * 3 + k) * C
                xc[r * 256 : (r + 1) * 256, at : at + C] = cot[r + 2 - b, 2 - k : 18 - k].reshape(256, C)
    quarter = (iota((512, C), 0) >> 2) & 3
    extra = nn(shifted[...], xc[:, 7 * C :])
    for pair in range(4):
        tiles = (2 * pair, 2 * pair + 1) if pair < 3 else (6,)
        totals = nn(shifted[...], xc[:, 2 * pair * C : min(2 * pair + 2, 7) * C])
        for at, tile in enumerate(tiles):
            total = totals[:, at * C : (at + 1) * C]
            if tile < 6:
                late = extra[:, (tile // 3) * C : (tile // 3 + 1) * C]
                total = jnp.where(quarter == 3, pltpu.roll(late, 12 - 4 * (tile % 3), 0), total)
            conv.grads[:, :, :, :, tile * C : (tile + 1) * C] = total.astype(BF).reshape(4, 4, 2, 16, C)
    conv.grads[:, :, :, :, 7 * C :] = jnp.zeros((4, 4, 2, 16, C), BF)
    conv.start_core()
    for r in range(4):
        terms = nt(xc[r * 256 : (r + 1) * 256], wb[...])
        grad = terms[:, 2 * C :] + later_frames(terms[:, C : 2 * C], 1) + later_frames(terms[:, :C], 2)
        i, a = r // 2, r % 2
        for j in range(8):
            at = (i * 8 + j) * 16
            pre_pair = pre[at : at + 16, 2 * a * C : (2 * a + 2) * C]
            gate = 1.0 / (1.0 + jnp.exp(-pre_pair))
            slope = gate * (1.0 + pre_pair * (1.0 - gate))
            pair = jnp.concatenate([grad[2 * j * 16 : 2 * j * 16 + 16], grad[2 * j * 16 + 16 : 2 * j * 16 + 32]], axis=1)
            grad_pre[at : at + 16, 2 * a * C : (2 * a + 2) * C] = (pair * slope).astype(BF)
    conv.start_first()

    grad_merged[...] = nt(grad_pre[...], wup[...])
    low = grad_merged[...].astype(BF)
    grad_mixed = nt(low, wout[...]).astype(BF)
    grad_joined[:, 2 * E :] = tn(probs[...].astype(BF), grad_mixed).astype(BF)
    grad_probs = nt(grad_mixed, values[...])
    inner = jnp.sum(probs[...] * grad_probs, axis=-1, keepdims=True)
    grad_scores = (probs[...] * (grad_probs - inner) * ROOT).astype(BF)
    grad_joined[:, :E] = norm_back(q_raw[...], nn(grad_scores, keys[...])).astype(BF)
    grad_joined[:, E : 2 * E] = norm_back(k_raw[...], tn(grad_scores, query[...])).astype(BF)
    qk.grads[...] = tn(normed[...], grad_joined[:, : 2 * E]).astype(BF).reshape(4, 4, 2, 16, 2 * E)
    qk.start_core()
    rest.grads[:, :, :, :, :E] = tn(merged[...], grad_pre[...]).astype(BF).reshape(4, 4, 2, 16, E)
    rest.grads[:, :, :, :, E : 2 * E] = tn(mixed[...], low).astype(BF).reshape(4, 4, 2, 16, E)
    rest.grads[:, :, :, :, 2 * E :] = tn(normed[...], grad_joined[:, 2 * E :]).astype(BF).reshape(4, 4, 2, 16, E)
    rest.start_core()

    grad_normed = nt(grad_joined[...], wqkv[...])
    states = norm_back(hs_send[...].reshape(256, E).astype(F32), grad_normed * gain_in[...])
    states = (grad_merged[...] + states).astype(BF)
    gs_send[...] = move(swap, states).reshape(8, 2, 16, E)
    qk.start_first()
    rest.start_first()
    gs_copies = exchange(2, lambda to: gs_send.at[to], gs_recv, mine)
    gs_recv[mine] = gs_send[t]
    pix_halo.finish()
    for r in range(4):
        taps = [pix[r + b, k : k + 16].reshape(256, C) for b in range(3) for k in range(3)]
        terms = nn(jnp.concatenate(taps, axis=1), wf[...])
        cells = terms[:, 2 * C :] + earlier_frames(terms[:, C : 2 * C], 1) + earlier_frames(terms[:, :C], 2)
        dec_send[:, :, r] = move(swap, cells.astype(BF)).reshape(8, 2, 16, C)
    dec_copies = exchange(3, lambda to: dec_send.at[to], dec_recv, mine)
    dec_recv[mine] = dec_send[t]
    conv.start_second()
    qk.start_second()
    rest.start_second()
    conv.start_rows()
    qk.start_rows()
    rest.start_rows()
    conv.start_gather()
    qk.start_gather()
    rest.start_gather()
    for copy in gs_copies:
        copy.wait()
    states_out[...] = gs_recv[...]
    for copy in dec_copies:
        copy.wait()
    dec_out[...] = dec_recv[...]
    conv.wait()
    rest.wait()
    conv_out[...] = conv.total[...]
    rest_out[...] = rest.total[...]
    qk.wait()
    qk_out[...] = qk.total[...]


GROUPS = ((1024, 2), (1536, 2), (1024, 3))
SHARES = (
    jax.ShapeDtypeStruct((16, 1536), F32),
    jax.ShapeDtypeStruct((16, 512), F32),
    jax.ShapeDtypeStruct((16, 512), F32),
    jax.ShapeDtypeStruct((27, 4, 128), F32),
)


def finish_kernel(dec, states, conv_sum, rest_sum, qk_sum, decoded_out, states_out, qkv_out, out_out, up_out, conv_out):
    token_scale = 1.0 / 65536.0**0.5
    voxel_scale = 1.0 / 262144.0**0.5
    from_blocks = from_blocks_matrix()
    for f in range(2):
        states_out[f] = move(from_blocks, states[:, f].reshape(128, E)).reshape(2, 64, E)
    for k in range(8):
        decoded_out[:, :, k * 16 : (k + 1) * 16, :] = dec[k]

    def tile_of(total, tile):
        count = total.shape[2] // 128
        at = (tile % count) * 128
        return total[tile // count][:, at : at + 128].astype(F32)

    for tile in range(8):
        qkv_out[:, tile * 128 : (tile + 1) * 128] = tile_of(qk_sum, tile) * token_scale
    for tile in range(4):
        up_out[:, tile * 128 : (tile + 1) * 128] = tile_of(rest_sum, tile) * token_scale
        out_out[:, tile * 128 : (tile + 1) * 128] = tile_of(rest_sum, 4 + tile) * token_scale
        qkv_out[:, 2 * E + tile * 128 : 2 * E + (tile + 1) * 128] = tile_of(rest_sum, 8 + tile) * token_scale
    for tile in range(7):
        block = tile_of(conv_sum, tile) * voxel_scale
        for kind in range(4):
            piece = block[kind * 4 : kind * 4 + 4]
            if kind < 3:
                conv_out[kind * 9 + tile] = piece
            elif tile < 6:
                conv_out[(tile % 3) * 9 + 7 + tile // 3] = piece


def body(hidden_states, attn_gain, qkv_weight, out_weight, up_weight, conv_weight, cotangent):
    vmem = pl.BlockSpec(memory_space=pltpu.VMEM)
    hbm = pl.BlockSpec(memory_space=pl.ANY)
    scratch = [
        pltpu.VMEM((2, 2, 64, E), BF),
        pltpu.VMEM((8, 2, 16, E), BF),
        pltpu.VMEM((8, 2, 16, E), BF),
        pltpu.VMEM((8, 2, 4, 16, C), BF),
        pltpu.VMEM((E, 3 * E), BF),
        pltpu.VMEM((E, E), BF),
        pltpu.VMEM((E, E), BF),
        pltpu.VMEM((27, C, C), BF),
        pltpu.VMEM((9 * C, 3 * C), BF),
        pltpu.VMEM((3 * C, 9 * C), BF),
        pltpu.VMEM((6, 18, 16, C), BF),
        pltpu.VMEM((6, 18, 16, C), BF),
        pltpu.VMEM((1024, 9 * C), BF),
        pltpu.VMEM((E, 1024), BF),
        pltpu.VMEM((256, E), BF),
        pltpu.VMEM((256, E), F32),
        pltpu.VMEM((256, E), F32),
        pltpu.VMEM((256, E), BF),
        pltpu.VMEM((256, E), BF),
        pltpu.VMEM((256, E), BF),
        pltpu.VMEM((256, 256), F32),
        pltpu.VMEM((256, E), BF),
        pltpu.VMEM((256, E), BF),
        pltpu.VMEM((256, E), F32),
        pltpu.VMEM((256, E), BF),
        pltpu.VMEM((256, E), F32),
        pltpu.VMEM((256, 3 * E), BF),
        pltpu.VMEM((8, 2, 4, 16, C), BF),
        pltpu.VMEM((8, 2, 4, 16, C), BF),
        pltpu.VMEM((8, 2, 16, E), BF),
        pltpu.VMEM((8, 2, 16, E), BF),
        pltpu.SemaphoreType.DMA((6,)),
        pltpu.SemaphoreType.DMA((4, 7)),
        pltpu.SemaphoreType.DMA((4, 7)),
        pltpu.SemaphoreType.DMA((2, 8)),
        pltpu.SemaphoreType.DMA((2, 8)),
    ]
    arrived = (
        jax.ShapeDtypeStruct((8, 2, 4, 16, C), BF),
        jax.ShapeDtypeStruct((8, 2, 16, E), BF),
    ) + tuple(jax.ShapeDtypeStruct((4, 16, width // 4), BF) for width, _ in GROUPS)
    results = pl.pallas_call(
        block_kernel,
        out_shape=arrived,
        in_specs=[hbm, vmem, hbm, hbm, hbm, hbm, hbm],
        out_specs=[vmem] * 5,
        scratch_shapes=scratch + [buffer for group in GROUPS for buffer in reducer_scratch(*group)],
        compiler_params=pltpu.CompilerParams(
            collective_id=0, has_side_effects=True, vmem_limit_bytes=56 * 2**20
        ),
    )(
        hidden_states,
        attn_gain.reshape(1, E),
        qkv_weight,
        out_weight,
        up_weight,
        conv_weight.reshape(27, C, C),
        cotangent,
    )
    decoded, states, qkv, out, up, conv = pl.pallas_call(
        finish_kernel,
        out_shape=(
            jax.ShapeDtypeStruct(cotangent.shape, BF),
            jax.ShapeDtypeStruct(hidden_states.shape, BF),
        )
        + SHARES,
        in_specs=[vmem] * 5,
        out_specs=[vmem] * 6,
    )(*results)
    return (decoded, states, qkv, out, up, conv.reshape(3, 3, 3, 4, C))


def solution(mesh):
    placed = (P("tm", "height", None, None), P(), P(), P(), P(), P(), P("tm", "height", None, None))
    return jax.shard_map(
        body,
        mesh=mesh,
        in_specs=placed,
        out_specs=(
            P("tm", "height", None, None),
            P("tm", "height", None, None),
            P("height", None),
            P("height", None),
            P("height", None),
            P(None, None, None, "height", None),
        ),
        check_vma=False,
    )
```
